256 devices in a mesh: seq: 32 (over y, x, core), head: 8 (over z).
Axes of the slice: x: 4, y: 4, z: 8, core: 2. Of those that a mesh axis runs over, the one named last changes fastest.
Arguments:
- query_in: bfloat16 [16384, 2048], P(('seq', 'head')), may hold values from -6 to 6
- key_in: bfloat16 [16384, 2048], P(('seq', 'head')), may hold values from -6 to 6
- value_in: bfloat16 [16384, 4096], P(('seq', 'head')), may hold values from -6 to 6
- gate_in: bfloat16 [16384, 4096], P(('seq', 'head')), may hold values from -6 to 6
- write_strength: bfloat16 [16384, 32], P(('seq', 'head')), may hold values from 0.0003 to 0.9
- log_decay: bfloat16 [16384, 32], P(('seq', 'head')), may hold values from -0.9 to 0
- conv_weight: bfloat16 [4, 8192], replicated, may hold values from -3 to 3
- norm_gain: float32 [128], replicated, may hold values from 0.1 to 1.9
Outputs:
- mixed: bfloat16 [16384, 4096], P(('seq', 'head'))
The draws below stay inside these ranges and needn't reach their ends.
All inputs are finite; a program needn't handle non-finite values.
Results may differ from the reference program's by a relative error of at most 0.0057.
Values may be sent and summed in bfloat16 or wider, within the bound.
A program may use at most 128 MiB of HBM per device.

```python
import jax
import jax.numpy as jnp
from jax import lax

HK = 16
VALUE_HEADS = 32
DK = 128
DV = 128
KERNEL = 4
SPAN = 64
TOK_DEV = 64
SEQUENCE_TOKENS = 16384


def head_classes(key, fast_count, strong_count):
    ranking = jax.random.permutation(key, VALUE_HEADS)
    return jnp.where(ranking < fast_count, 0, jnp.where(ranking < fast_count + strong_count, 1, 2))


def draw_write_strength(key, part):
    fast_count = VALUE_HEADS // 4
    classes = head_classes(key, fast_count, VALUE_HEADS // 4)
    key = jax.random.fold_in(key, 11)
    random_keys = jax.random.split(key, 2)
    weak_write = jnp.exp(jax.random.uniform(random_keys[0], (SEQUENCE_TOKENS, VALUE_HEADS), jnp.float32, jnp.log(0.0003), jnp.log(0.01)))
    strong = jnp.exp(jax.random.uniform(random_keys[1], (SEQUENCE_TOKENS, VALUE_HEADS), jnp.float32, jnp.log(0.1), jnp.log(0.9)))
    return jnp.where((classes == 2)[None, :], weak_write, strong).astype(jnp.bfloat16)


def draw_log_decay(key, part):
    fast_count = VALUE_HEADS // 4
    classes = head_classes(key, fast_count, VALUE_HEADS // 4)
    key = jax.random.fold_in(key, 23)
    random_keys = jax.random.split(key, 6)
    fast_rate = jnp.exp(jax.random.uniform(random_keys[0], (VALUE_HEADS,), jnp.float32, jnp.log(1.0 / 50.0), jnp.log(1.0 / 30.0)))
    slow_rate = jnp.exp(jax.random.uniform(random_keys[1], (VALUE_HEADS,), jnp.float32, jnp.log(0.1), jnp.log(0.6))) / SEQUENCE_TOKENS
    single_token_update = jnp.where(classes == 0, fast_rate, slow_rate)
    random_noise = jnp.exp(jax.random.uniform(random_keys[2], (SEQUENCE_TOKENS, VALUE_HEADS), jnp.float32, jnp.log(0.5), jnp.log(2.0)))
    local_section = jnp.exp(jax.random.uniform(random_keys[3], (SEQUENCE_TOKENS // TOK_DEV, 1, VALUE_HEADS), jnp.float32, jnp.log(0.5), jnp.log(2.0)))
    local_section = jnp.broadcast_to(local_section, (SEQUENCE_TOKENS // TOK_DEV, TOK_DEV, VALUE_HEADS)).reshape(SEQUENCE_TOKENS, VALUE_HEADS)
    token_groups = jax.random.uniform(random_keys[4], (SEQUENCE_TOKENS, VALUE_HEADS)) < 2.0 / SEQUENCE_TOKENS
    retained_fraction = jax.random.uniform(random_keys[5], (SEQUENCE_TOKENS, VALUE_HEADS), jnp.float32, 0.5, 0.8)
    value_vectors = -single_token_update[None, :] * random_noise * local_section + jnp.where(token_groups, jnp.log(retained_fraction), 0.0)
    return value_vectors.astype(jnp.bfloat16)


def levels(own_key, extent, cuts, smallest, high):
    loudness = 1.0
    for axis_at, blocks in cuts:
        steps = jax.random.uniform(jax.random.fold_in(jax.random.fold_in(own_key, 6), axis_at), (blocks,), jnp.float32, smallest / len(cuts), high / len(cuts))
        loudness = loudness * jnp.repeat(jnp.exp(steps), extent[axis_at] // blocks).reshape((-1,) + (1,) * (len(extent) - 1 - axis_at))
    return loudness


def noise(stream_key, extent, width, bound, shards=(), kind=jnp.bfloat16):
    loudness = levels(stream_key, extent, shards, -0.22, 0.18) if shards else 1.0
    drawn = jax.random.normal(stream_key, extent, jnp.float32) * width * loudness
    return jnp.minimum(jnp.maximum(drawn, -bound), bound).astype(kind)


def setup_inputs(seed: int = 0) -> dict:
    keys = jax.random.split(jax.random.key(seed), 9)
    return {
        "query_in": noise(keys[0], (SEQUENCE_TOKENS, HK * DK), 1.0, 6.0, ((0, 256),)),
        "key_in": noise(keys[1], (SEQUENCE_TOKENS, HK * DK), 1.0, 6.0, ((0, 256),)),
        "value_in": noise(keys[2], (SEQUENCE_TOKENS, VALUE_HEADS * DV), 1.0, 6.0, ((0, 256),)),
        "gate_in": noise(keys[3], (SEQUENCE_TOKENS, VALUE_HEADS * DV), 1.0, 6.0, ((0, 256),)),
        "write_strength": draw_write_strength(jax.random.fold_in(keys[8], 71), 0),
        "log_decay": draw_log_decay(jax.random.fold_in(keys[8], 71), 0),
        "conv_weight": noise(keys[6], (KERNEL, 2 * HK * DK + VALUE_HEADS * DV), KERNEL ** -0.5, 3.0),
        "norm_gain": jnp.clip(1.0 + 0.18 * jax.random.normal(keys[7], (DV,), jnp.float32), 0.1, 1.9),
    }


exact_precision = lax.Precision.HIGHEST
EPSILON = 1e-06

def causal_conv(inputs, before, weights):
    length = inputs.shape[0]
    padded = jnp.concatenate([before, inputs], axis=0)
    running = jnp.zeros(inputs.shape, jnp.float32)
    for offset in range(weights.shape[0]):
        running = running + padded[offset:offset + length].astype(jnp.float32) * weights[offset].astype(jnp.float32)
    return jax.nn.silu(running).astype(jnp.bfloat16)

def split_heads(source, head_count):
    row_count = source.shape[0]
    value_vectors = lax.optimization_barrier(source).astype(jnp.float32).reshape(row_count, head_count, -1)
    return jnp.transpose(value_vectors, (1, 0, 2))

def unit_rows(value_vectors):
    return value_vectors * lax.rsqrt(lax.optimization_barrier(jnp.sum(value_vectors * value_vectors, axis=-1, keepdims=True)) + EPSILON)

def unit_inverse(lower_part):
    block_rows = lower_part.shape[-1]
    identity = jnp.eye(block_rows, dtype=jnp.float32)
    power = -lower_part
    inverse = identity + power
    for level in range(1, max(1, (block_rows - 1).bit_length())):
        power = jnp.einsum('...ij,...jk->...ik', power, power, precision=exact_precision)
        inverse = jnp.einsum('...ij,...jk->...ik', inverse, identity + power, precision=exact_precision)
    return inverse

def block_terms(queries, keys_unit, value_vectors, strength, decays):
    block_rows = queries.shape[-2]
    cumulative = jnp.cumsum(decays, axis=-1)
    spread = cumulative[..., :, None] - cumulative[..., None, :]
    rowpos = lax.broadcasted_iota(jnp.int32, (block_rows, block_rows), 0)
    colpos = lax.broadcasted_iota(jnp.int32, (block_rows, block_rows), 1)
    strictly = rowpos > colpos
    within = rowpos >= colpos
    fading = jnp.where(within, jnp.exp(jnp.where(within, spread, 0.0)), 0.0)
    intersection = jnp.einsum('...id,...jd->...ij', keys_unit, keys_unit, precision=exact_precision)
    lower_part = jnp.where(strictly, intersection * fading * strength[..., :, None], 0.0)
    inverse = unit_inverse(lower_part)
    erase_rows = jnp.einsum('...ij,...jd->...id', inverse, keys_unit * (strength * jnp.exp(cumulative))[..., None], precision=exact_precision)
    write_rows = jnp.einsum('...ij,...jd->...id', inverse, value_vectors * strength[..., None], precision=exact_precision)
    ending = cumulative[..., -1:]
    key_end = keys_unit * jnp.exp(ending - cumulative)[..., None]
    query_decayed = queries * jnp.exp(cumulative)[..., None]
    scores = jnp.einsum('...id,...jd->...ij', queries, keys_unit, precision=exact_precision) * fading
    return (erase_rows, write_rows, key_end, query_decayed, scores, jnp.exp(ending[..., 0]))

def advance(pieces, carried):
    erase_rows, write_rows, key_end, query_decayed, scores, falloff = pieces
    fresh_rows = write_rows - jnp.einsum('...ik,...kv->...iv', erase_rows, carried, precision=exact_precision)
    attended = jnp.einsum('...ik,...kv->...iv', query_decayed, carried, precision=exact_precision) + jnp.einsum('...ij,...jv->...iv', scores, fresh_rows, precision=exact_precision)
    carried = falloff[..., None, None] * carried + jnp.einsum('...ik,...iv->...kv', key_end, fresh_rows, precision=exact_precision)
    return (attended, carried)

def gated_norm(attended, gate_rows, norm_gain):
    row_count = attended.shape[0]
    value_vectors = lax.optimization_barrier(attended).astype(jnp.float32).reshape(row_count, -1, norm_gain.shape[0])
    value_vectors = value_vectors * lax.rsqrt(lax.optimization_barrier(jnp.mean(value_vectors * value_vectors, axis=-1, keepdims=True)) + EPSILON)
    gating = jax.nn.silu(gate_rows.astype(jnp.float32)).reshape(value_vectors.shape)
    return (value_vectors * norm_gain * gating).reshape(row_count, -1).astype(jnp.bfloat16)

def reference(query_in, key_in, value_in, gate_in, write_strength, log_decay, conv_weight, norm_gain):
    blocks = SEQUENCE_TOKENS // SPAN
    rim_rows = KERNEL - 1
    key_cols = HK * DK
    repeat = VALUE_HEADS // HK
    streams = (query_in.reshape(blocks, SPAN, -1), key_in.reshape(blocks, SPAN, -1), value_in.reshape(blocks, SPAN, -1), gate_in.reshape(blocks, SPAN, -1), write_strength.reshape(blocks, SPAN, VALUE_HEADS), log_decay.reshape(blocks, SPAN, VALUE_HEADS))
    query_weights = conv_weight[:, :key_cols]
    key_weights = conv_weight[:, key_cols:2 * key_cols]
    value_weights = conv_weight[:, 2 * key_cols:]

    def advance_block(carried, current):
        recurrent_state, query_tail, key_tail, value_tail = carried
        query_raw, key_raw, value_raw, gate_rows, strength, decays = current
        queries = unit_rows(split_heads(causal_conv(query_raw, query_tail, query_weights), HK)) * DK ** (-0.5)
        keys_unit = unit_rows(split_heads(causal_conv(key_raw, key_tail, key_weights), HK))
        value_vectors = split_heads(causal_conv(value_raw, value_tail, value_weights), VALUE_HEADS)
        queries = jnp.repeat(queries, repeat, axis=0)
        keys_unit = jnp.repeat(keys_unit, repeat, axis=0)
        pieces = block_terms(queries, keys_unit, value_vectors, strength.astype(jnp.float32).T, decays.astype(jnp.float32).T)
        attended, recurrent_state = advance(pieces, recurrent_state)
        attended = jnp.transpose(attended, (1, 0, 2)).reshape(SPAN, VALUE_HEADS * DV).astype(jnp.bfloat16)
        mixed_rows = gated_norm(attended, gate_rows, norm_gain)
        return ((recurrent_state, query_raw[SPAN - rim_rows:], key_raw[SPAN - rim_rows:], value_raw[SPAN - rim_rows:]), mixed_rows)
    initial = (jnp.zeros((VALUE_HEADS, DK, DV), jnp.float32), jnp.zeros((rim_rows, key_cols), jnp.bfloat16), jnp.zeros((rim_rows, key_cols), jnp.bfloat16), jnp.zeros((rim_rows, VALUE_HEADS * DV), jnp.bfloat16))
    _, mixed = lax.scan(advance_block, initial, streams)
    return mixed.reshape(SEQUENCE_TOKENS, VALUE_HEADS * DV)
```

```python
import functools

import jax
import jax.numpy as jnp
from jax import lax
from jax.experimental import pallas as pl
from jax.experimental.pallas import tpu as pltpu
from jax.sharding import PartitionSpec as P

MESH = pl.DeviceIdType.MESH
F32 = jnp.float32
BF16 = jnp.bfloat16
EPSILON = 1e-06

GROUPS = 8
TOK = 64
LINE = 8
LINES = 4
SEQ = LINE * LINES
HEADS = 4
D = 128
C = 128
ROWS = TOK * GROUPS
CHUNKS = ROWS // C
RIM = 16

NN = (((1,), (0,)), ((), ()))
NT = (((1,), (1,)), ((), ()))
TN = (((0,), (0,)), ((), ()))


def dot(a, b, dims=NN):
    return lax.dot_general(a, b, dims, preferred_element_type=F32)


def split(x):
    high = x.astype(BF16)
    return high, (x - high.astype(F32)).astype(BF16)


def mm3(a, b, dims=NN):
    a1, a2 = split(a)
    b1, b2 = split(b)
    return dot(a1, b1, dims) + (dot(a1, b2, dims) + dot(a2, b1, dims))


def mm2l(a, b, dims=NN):
    a1, a2 = split(a)
    return dot(a1, b, dims) + dot(a2, b, dims)


def mm2r(a, b, dims=NN):
    b1, b2 = split(b)
    return dot(a, b1, dims) + dot(a, b2, dims)


def mm1(a, b, dims=NN):
    return dot(a.astype(BF16), b.astype(BF16), dims)


def silu(x):
    return x / (1.0 + jnp.exp(-x))


def conv(buf, start, taps):
    x = buf[pl.ds(start, C + RIM), :].astype(F32)
    total = x[RIM - 3 : RIM - 3 + C] * taps[0:1]
    for j in range(1, 4):
        total = total + x[RIM - 3 + j : RIM - 3 + j + C] * taps[j : j + 1]
    return silu(total).astype(BF16)


def unit_inverse(lower, rows, cols):
    t = jnp.where(rows == cols, 1.0, 0.0).reshape(C // 8, 8, C)
    base = (rows // 8) * 8
    for j in range(7):
        factor = jnp.sum(jnp.where(cols == base + j, lower, 0.0), axis=1, keepdims=True)
        t = t - factor.reshape(C // 8, 8, 1) * t[:, j : j + 1, :]
    t = t.reshape(C, C)
    size = 8
    while size < C:
        below = (rows // size == cols // size + 1) & (rows // size % 2 == 1)
        part = jnp.where(below, lower, 0.0)
        t = t - mm3(t, mm3(part, t))
        size *= 2
    return t


def kernel(
    q_in, k_in, v_in, gate_in, ws_in, ld_in, w_in, gain_ref, out_ref,
    qbuf, kbuf, vbuf, gate, ws, ld, wbuf, gb_send, gb_recv,
    kc, fs, tinv, ew, mc, ac, pre, m_send, a_send, m_recv, a_recv,
    mpre, msuf, apre, ym_send, ya_send, ym_recv, ya_recv, h_send, h_recv, pb, o_send, o_recv,
    local_sem, send_sem, recv_sem,
):
    s = lax.axis_index("seq")
    z = lax.axis_index("head")
    y = s // LINE
    l = lax.rem(s, LINE)

    def at_head(d):
        return lax.rem(z + d, GROUPS)

    def at_line(d):
        return lax.rem(l + d, LINE)

    barrier = pltpu.get_barrier_semaphore()
    for d in range(1, GROUPS):
        pl.semaphore_signal(barrier, inc=1, device_id=(s, at_head(d)), device_id_type=MESH)
    for d in range(1, LINE):
        pl.semaphore_signal(barrier, inc=1, device_id=(y * LINE + at_line(d), z), device_id_type=MESH)
    for d in range(1, LINES):
        pl.semaphore_signal(
            barrier, inc=1, device_id=(lax.rem(y + d, LINES) * LINE + l, z), device_id_type=MESH
        )
    pl.semaphore_signal(barrier, inc=1, device_id=(lax.rem(s + SEQ - 1, SEQ), z), device_id_type=MESH)

    mine = pl.ds(pl.multiple_of(RIM + z * TOK, RIM), TOK)

    def own_columns(width):
        return pl.ds(pl.multiple_of(z * width, width), width)

    copies = [
        pltpu.make_async_copy(ws_in, ws, local_sem.at[0]),
        pltpu.make_async_copy(ld_in, ld, local_sem.at[1]),
        pltpu.make_async_copy(w_in, wbuf, local_sem.at[2]),
        pltpu.make_async_copy(k_in.at[:, own_columns(256)], kbuf.at[mine, :], local_sem.at[3]),
        pltpu.make_async_copy(v_in.at[:, own_columns(512)], vbuf.at[mine, :], local_sem.at[4]),
        pltpu.make_async_copy(q_in.at[:, own_columns(256)], qbuf.at[mine, :], local_sem.at[5]),
        pltpu.make_async_copy(gate_in, gate, local_sem.at[6]),
    ]
    for copy in copies:
        copy.start()

    rows = lax.broadcasted_iota(jnp.int32, (C, C), 0)
    cols = lax.broadcasted_iota(jnp.int32, (C, C), 1)
    eye = rows == cols
    tril = rows >= cols
    strict = rows > cols

    copies[0].wait()
    copies[1].wait()
    upto = jnp.where(tril[:TOK, :TOK], 1.0, 0.0).astype(BF16)
    running = dot(upto, ld[...])
    both = jnp.concatenate([ws[...].astype(F32), running], axis=1)
    both = jnp.concatenate([both, both], axis=0).T
    for g in range(GROUPS):
        gb_send[g] = jnp.concatenate(
            [both[HEADS * g : HEADS * g + HEADS], both[32 + HEADS * g : 32 + HEADS * g + HEADS]], axis=0
        )
    pl.semaphore_wait(barrier, GROUPS - 1 + LINE - 1 + LINES - 1 + 1)

    def to_head(kind, d, src, dst):
        return pltpu.make_async_remote_copy(
            src_ref=src,
            dst_ref=dst,
            send_sem=send_sem.at[kind, d],
            recv_sem=recv_sem.at[kind, d],
            device_id=(s, at_head(d)),
            device_id_type=MESH,
        )

    def to_seq(kind, d, target, src, dst):
        return pltpu.make_async_remote_copy(
            src_ref=src,
            dst_ref=dst,
            send_sem=send_sem.at[kind, d],
            recv_sem=recv_sem.at[kind, d],
            device_id=(target, z),
            device_id_type=MESH,
        )

    def columns_to(d, width):
        return pl.ds(pl.multiple_of(at_head(d) * width, width), width)

    order = [4, 3, 5, 2, 6, 1, 7]
    k_copies, v_copies, q_copies, g_copies = [], [], [], []
    for d in order:
        g_copies.append(to_head(0, d, gb_send.at[at_head(d)], gb_recv.at[z]))
        k_copies.append(to_head(1, d, k_in.at[:, columns_to(d, 256)], kbuf.at[mine, :]))
    for d in order:
        v_copies.append(to_head(2, d, v_in.at[:, columns_to(d, 512)], vbuf.at[mine, :]))
    for d in order:
        q_copies.append(to_head(3, d, q_in.at[:, columns_to(d, 256)], qbuf.at[mine, :]))
    for copy in g_copies + k_copies + v_copies + q_copies:
        copy.start()
    gb_recv[z] = gb_send[z]

    following = lax.rem(s + 1, SEQ)

    def rim_copy(index, buf):
        return to_seq(4, index, following, buf.at[pl.ds(ROWS, RIM), :], buf.at[pl.ds(0, RIM), :])

    def arrived(own, others, index, buf):
        own.wait()
        for copy in others:
            copy.wait_recv()
        rim = rim_copy(index, buf)
        rim.start()
        return rim

    def rim_arrived(rim, buf):
        rim.wait_recv()

        @pl.when(s == 0)
        def _():
            buf[pl.ds(0, RIM), :] = jnp.zeros((RIM, buf.shape[1]), BF16)

    def chunk_scales(c):
        first, second = gb_recv[2 * c], gb_recv[2 * c + 1]
        lane = lax.broadcasted_iota(jnp.int32, (8, C), 1)
        sub = lax.broadcasted_iota(jnp.int32, (8, C), 0)
        carry = jnp.where(sub >= HEADS, first[:, TOK - 1 : TOK], 0.0)
        across = jnp.where(lane < TOK, first, second + carry)
        return across, across.T

    copies[2].wait()
    for copy in g_copies:
        copy.wait_recv()
    k_rim = arrived(copies[3], k_copies, 0, kbuf)
    rim_arrived(k_rim, kbuf)
    taps_k = wbuf[:, pl.ds(pl.multiple_of(2048 + z * 256, 256), 256)].astype(F32)

    def key_body(i, carry):
        c = lax.rem(i + 1, CHUNKS)
        start = pl.multiple_of(c * C, C)
        block = pl.ds(start, C)
        keys = conv(kbuf, start, taps_k)
        kc[block, :] = keys
        across, down = chunk_scales(c)
        for kh in range(2):
            key = keys[:, kh * D : (kh + 1) * D]
            kk = dot(key, key, NT)
            diagonal = jnp.where(eye, kk, 0.0)
            s_col = lax.rsqrt(jnp.sum(diagonal, axis=1, keepdims=True) + EPSILON)
            s_row = lax.rsqrt(jnp.sum(diagonal, axis=0, keepdims=True) + EPSILON)
            for j in range(2):
                h = kh * 2 + j
                b_col, c_col = down[:, h : h + 1], down[:, HEADS + h : HEADS + h + 1]
                b_row, c_row = across[h : h + 1], across[HEADS + h : HEADS + h + 1]
                fade = jnp.where(tril, jnp.exp(jnp.where(tril, c_col - c_row, 0.0)), 0.0) * s_row
                fs[h, block, :] = fade
                lower = jnp.where(strict, kk * fade * (s_col * b_col), 0.0)
                t = unit_inverse(lower, rows, cols) * b_row
                tinv[h, block, :] = t
                erase = mm2l(t * (s_row * jnp.exp(c_row)), key)
                ew[h, block, pl.ds(0, D)] = erase
                end = c_row[:, C - 1 : C]
                taken = mm2r(key, erase * (s_col * jnp.exp(end - c_col)), TN)
                mc[h, c] = jnp.where(eye, jnp.exp(end), 0.0) - taken
        return carry

    lax.fori_loop(0, CHUNKS, key_body, 0)

    identity = jnp.where(eye, 1.0, 0.0)
    left, right = pl.ds(0, D), pl.ds(D, D)
    for h in range(HEADS):
        pre[h, 0, :, left] = identity
        pre[h, 0, :, right] = jnp.zeros((D, D), F32)
        running = mc[h, 0]
        for c in range(1, CHUNKS):
            pre[h, c, :, left] = running
            running = mm3(mc[h, c], running)
        m_send[h] = running

    def unit_head(u):
        return u // 2

    def unit_half(u):
        return pl.ds(pl.multiple_of(lax.rem(u, 2) * 64, 64), 64)

    m_copies, a_copies, h_copies = [], [], []
    for d in range(1, LINE):
        u = at_line(d)
        target = y * LINE + u
        m_copies.append(to_seq(5, d, target, m_send.at[unit_head(u)], m_recv.at[l]))
        a_copies.append(to_seq(6, d, target, a_send.at[unit_head(u), unit_half(u), :], a_recv.at[l]))
        h_copies.append(to_seq(7, d, target, h_send.at[u], h_recv.at[l]))
    for copy in m_copies:
        copy.start()
    m_recv[l] = m_send[unit_head(l)]

    v_rim = arrived(copies[4], v_copies, 1, vbuf)
    rim_arrived(v_rim, vbuf)
    taps_v = wbuf[:, pl.ds(pl.multiple_of(4096 + z * 512, 512), 512)].astype(F32)

    def value_body(c, carry):
        start = pl.multiple_of(c * C, C)
        block = pl.ds(start, C)
        values = conv(vbuf, start, taps_v)
        across, down = chunk_scales(c)
        for kh in range(2):
            key = kc[block, pl.ds(kh * D, D)]
            key32 = key.astype(F32)
            s_col = lax.rsqrt(jnp.sum(key32 * key32, axis=1, keepdims=True) + EPSILON)
            for j in range(2):
                h = kh * 2 + j
                c_col = down[:, HEADS + h : HEADS + h + 1]
                end = across[HEADS + h : HEADS + h + 1, C - 1 : C]
                write = mm2l(tinv[h, block, :], values[:, h * D : (h + 1) * D])
                ew[h, block, pl.ds(D, D)] = write
                ac[h, c] = mm2r(key, write * (s_col * jnp.exp(end - c_col)), TN)
        return carry

    lax.fori_loop(0, CHUNKS, value_body, 0)
    for h in range(HEADS):
        running = ac[h, 0]
        for c in range(1, CHUNKS):
            pre[h, c, :, right] = running
            running = mm3(mc[h, c], running) + ac[h, c]
        a_send[h] = running.T
    for copy in a_copies:
        copy.start()
    a_recv[l] = a_send[unit_head(l), unit_half(l), :]

    for copy in m_copies:
        copy.wait_recv()
    running = m_recv[0]
    for i in range(1, LINE):
        mpre[i] = running
        running = mm3(m_recv[i], running)
    ym_send[...] = running
    ym_copies, ya_copies = [], []
    for d in range(1, LINES):
        target = lax.rem(y + d, LINES) * LINE + l
        ym_copies.append(to_seq(8, d, target, ym_send, ym_recv.at[d - 1]))
        ya_copies.append(to_seq(9, d, target, ya_send, ya_recv.at[d - 1]))
    for copy in ym_copies:
        copy.start()
    running = m_recv[LINE - 1]
    for i in range(LINE - 2, -1, -1):
        msuf[i] = running
        if i:
            running = mm3(running, m_recv[i])

    for copy in a_copies:
        copy.wait_recv()
    total = a_recv[LINE - 1]
    for i in range(LINE - 1):
        total = total + mm3(a_recv[i], msuf[i], NT)
    ya_send[...] = total
    for copy in ya_copies:
        copy.start()

    running = a_recv[0]
    for i in range(1, LINE):
        apre[i] = running
        if i < LINE - 1:
            running = mm3(running, m_recv[i], NT) + a_recv[i]

    for copy in ym_copies:
        copy.wait_recv()
    across_two = mm3(ym_recv[0], ym_recv[1])
    for copy in ya_copies:
        copy.wait_recv()
    entering = jnp.where(y >= 1, ya_recv[0], 0.0)
    entering = entering + jnp.where(y >= 2, mm3(ya_recv[1], ym_recv[0], NT), 0.0)
    entering = entering + jnp.where(y >= 3, mm3(ya_recv[2], across_two, NT), 0.0)
    h_send[0] = entering
    for i in range(1, LINE):
        h_send[i] = mm3(entering, mpre[i], NT) + apre[i]
    for copy in h_copies:
        copy.start()
    h_recv[l] = h_send[l]

    q_rim = arrived(copies[5], q_copies, 2, qbuf)
    rim_arrived(q_rim, qbuf)
    taps_q = wbuf[:, pl.ds(pl.multiple_of(z * 256, 256), 256)].astype(F32)

    def query_body(c, carry):
        start = pl.multiple_of(c * C, C)
        block = pl.ds(start, C)
        queries = conv(qbuf, start, taps_q)
        across, down = chunk_scales(c)
        for kh in range(2):
            key = kc[block, pl.ds(kh * D, D)]
            query = queries[:, kh * D : (kh + 1) * D]
            query32 = query.astype(F32)
            s_col = lax.rsqrt(jnp.sum(query32 * query32, axis=1, keepdims=True) + EPSILON) * (D**-0.5)
            qk = dot(query, key, NT) * s_col
            for j in range(2):
                h = kh * 2 + j
                c_col = down[:, HEADS + h : HEADS + h + 1]
                inner = mm3(qk * fs[h, block, :], ew[h, block, :])
                reads = query32 * (s_col * jnp.exp(c_col)) - inner[:, :D]
                outer = mm3(reads, pre[h, c])
                pb[h, block, left] = outer[:, :D]
                pb[h, block, right] = outer[:, D:] + inner[:, D:]
        return carry

    lax.fori_loop(0, CHUNKS, query_body, 0)

    for copy in h_copies:
        copy.wait_recv()
    o_copies = []
    for d in range(1, GROUPS):
        o_copies.append(to_head(10, d, o_send.at[at_head(d)], o_recv.at[z]))

    def out_rows(t):
        block = pl.ds(pl.multiple_of(t * TOK, TOK), TOK)
        for h in range(HEADS):
            state = jnp.concatenate([h_recv[2 * h], h_recv[2 * h + 1]], axis=0)
            o = mm3(pb[h, block, left], state, NT) + pb[h, block, right]
            o_send[t, :, pl.ds(h * D, D)] = o.astype(BF16)

    for copy, d in zip(o_copies, range(1, GROUPS)):
        out_rows(at_head(d))
        copy.start()
    out_rows(z)
    o_recv[z] = o_send[z]

    copies[6].wait()
    for copy in o_copies:
        copy.wait_recv()
    gain = gain_ref[...]

    def norm_body(g, carry):
        for h in range(HEADS):
            a = o_recv[g, :, pl.ds(h * D, D)].astype(F32)
            a = a * lax.rsqrt(jnp.mean(a * a, axis=1, keepdims=True) + EPSILON)
            here = pl.ds(pl.multiple_of(g * 512 + h * D, D), D)
            out_ref[:, here] = (a * gain * silu(gate[:, here].astype(F32))).astype(BF16)
        return carry

    lax.fori_loop(0, GROUPS, norm_body, 0)

    for copy in g_copies + k_copies + v_copies + q_copies + [k_rim, v_rim, q_rim]:
        copy.wait_send()
    for copy in m_copies + a_copies + h_copies + ym_copies + ya_copies + o_copies:
        copy.wait_send()


def local(query_in, key_in, value_in, gate_in, write_strength, log_decay, conv_weight, norm_gain):
    anywhere = pl.BlockSpec(memory_space=pl.ANY)
    vmem = pl.BlockSpec(memory_space=pltpu.VMEM)
    return pl.pallas_call(
        kernel,
        out_shape=jax.ShapeDtypeStruct((TOK, 4096), BF16),
        in_specs=[anywhere] * 7 + [vmem],
        out_specs=vmem,
        scratch_shapes=[
            pltpu.VMEM((RIM + ROWS, 256), BF16),
            pltpu.VMEM((RIM + ROWS, 256), BF16),
            pltpu.VMEM((RIM + ROWS, 512), BF16),
            pltpu.VMEM((TOK, 4096), BF16),
            pltpu.VMEM((TOK, 32), BF16),
            pltpu.VMEM((TOK, 32), BF16),
            pltpu.VMEM((4, 8192), BF16),
            pltpu.VMEM((GROUPS, 8, C), F32),
            pltpu.VMEM((GROUPS, 8, C), F32),
            pltpu.VMEM((ROWS, 256), BF16),
            pltpu.VMEM((HEADS, ROWS, C), F32),
            pltpu.VMEM((HEADS, ROWS, C), F32),
            pltpu.VMEM((HEADS, ROWS, 2 * D), F32),
            pltpu.VMEM((HEADS, CHUNKS, D, D), F32),
            pltpu.VMEM((HEADS, CHUNKS, D, D), F32),
            pltpu.VMEM((HEADS, CHUNKS, D, 2 * D), F32),
            pltpu.VMEM((HEADS, D, D), F32),
            pltpu.VMEM((HEADS, D, D), F32),
            pltpu.VMEM((LINE, D, D), F32),
            pltpu.VMEM((LINE, 64, D), F32),
            pltpu.VMEM((LINE, D, D), F32),
            pltpu.VMEM((LINE, D, D), F32),
            pltpu.VMEM((LINE, 64, D), F32),
            pltpu.VMEM((D, D), F32),
            pltpu.VMEM((64, D), F32),
            pltpu.VMEM((LINES - 1, D, D), F32),
            pltpu.VMEM((LINES - 1, 64, D), F32),
            pltpu.VMEM((LINE, 64, D), F32),
            pltpu.VMEM((LINE, 64, D), F32),
            pltpu.VMEM((HEADS, ROWS, 2 * D), F32),
            pltpu.VMEM((GROUPS, TOK, 512), BF16),
            pltpu.VMEM((GROUPS, TOK, 512), BF16),
            pltpu.SemaphoreType.DMA((7,)),
            pltpu.SemaphoreType.DMA((11, 8)),
            pltpu.SemaphoreType.DMA((11, 8)),
        ],
        compiler_params=pltpu.CompilerParams(
            collective_id=0, has_side_effects=True, vmem_limit_bytes=48 * 1024 * 1024
        ),
    )(
        query_in, key_in, value_in, gate_in, write_strength, log_decay, conv_weight, norm_gain.reshape(1, D)
    )


def solution(mesh):
    rows = P(("seq", "head"), None)
    return jax.shard_map(
        local,
        mesh=mesh,
        in_specs=(rows, rows, rows, rows, rows, rows, P(), P()),
        out_specs=rows,
        check_vma=False,
    )
```

```python
import functools

import jax
import jax.numpy as jnp
from jax import lax
from jax.experimental import pallas as pl
from jax.experimental.pallas import tpu as pltpu
from jax.sharding import PartitionSpec as P

MESH = pl.DeviceIdType.MESH
F32 = jnp.float32
BF16 = jnp.bfloat16
EPSILON = 1e-06

GROUPS = 8
TOK = 64
LINE = 8
LINES = 4
SEQ = LINE * LINES
HEADS = 4
D = 128
C = 128
ROWS = TOK * GROUPS
CHUNKS = ROWS // C
RIM = 16

NN = (((1,), (0,)), ((), ()))
NT = (((1,), (1,)), ((), ()))
TN = (((0,), (0,)), ((), ()))


def dot(a, b, dims=NN):
    return lax.dot_general(a, b, dims, preferred_element_type=F32)


def split(x):
    high = x.astype(BF16)
    return high, (x - high.astype(F32)).astype(BF16)


def beside(b1, b2, dims):
    return jnp.concatenate([b1, b2], axis=0 if dims == NT else 1)


def mm2l(a, b, dims=NN):
    a1, a2 = split(a)
    axis = 1 if dims == NT else 0
    return dot(jnp.concatenate([a1, a2], axis=1), jnp.concatenate([b, b], axis=axis), dims)


def mm2r(a, b, dims=NN):
    b1, b2 = split(b)
    both = dot(a, beside(b1, b2, dims), dims)
    half = both.shape[1] // 2
    return both[:, :half] + both[:, half:]


def mm3(a, b, dims=NN):
    a1, a2 = split(a)
    b1, b2 = split(b)
    if b.shape[0 if dims == NT else 1] > D:
        axis = 1 if dims == NT else 0
        main = dot(jnp.concatenate([a1, a2], axis=1), jnp.concatenate([b1, b1], axis=axis), dims)
        return main + dot(a1, b2, dims)
    both = dot(a1, beside(b1, b2, dims), dims)
    half = both.shape[1] // 2
    return both[:, :half] + both[:, half:] + dot(a2, b1, dims)


def silu(x):
    return x / (1.0 + jnp.exp(-x))


def conv(buf, start, taps):
    x = buf[pl.ds(start, C + RIM), :].astype(F32)
    total = x[RIM - 3 : RIM - 3 + C] * taps[0:1]
    for j in range(1, 4):
        total = total + x[RIM - 3 + j : RIM - 3 + j + C] * taps[j : j + 1]
    return silu(total).astype(BF16)


def odd_blocks(x, size):
    return jnp.concatenate([x[i : i + size] for i in range(size, C, 2 * size)], axis=0)


def to_odd_blocks(x, size):
    zero = jnp.zeros((size, x.shape[1]), x.dtype)
    parts = []
    for i in range(0, C // 2, size):
        parts += [zero, x[i : i + size]]
    return jnp.concatenate(parts, axis=0)


def unit_inverses(lowers, rows, cols):
    identity = jnp.where(rows == cols, 1.0, 0.0)
    base = (rows // 8) * 8
    ts = [identity.reshape(C // 8, 8, C)] * len(lowers)
    for j in range(7):
        picked = cols == base + j
        for n, lower in enumerate(lowers):
            factor = jnp.sum(jnp.where(picked, lower, 0.0), axis=1, keepdims=True).reshape(C // 8, 8, 1)
            ts[n] = ts[n] - factor * ts[n][:, j : j + 1, :]
    ts = [t.reshape(C, C) for t in ts]
    size = 8
    while size < C:
        below = odd_blocks(cols // size, size) == odd_blocks(rows // size, size) - 1
        parts = [jnp.where(below, odd_blocks(lower, size), 0.0).astype(BF16) for lower in lowers]
        firsts = [dot(part, t.astype(BF16)) for part, t in zip(parts, ts)]
        seconds = [
            dot(odd_blocks(t, size).astype(BF16), to_odd_blocks(first, size).astype(BF16))
            for t, first in zip(ts, firsts)
        ]
        ts = [t - to_odd_blocks(second, size) for t, second in zip(ts, seconds)]
        size *= 2
    rounded = [t.astype(BF16) for t in ts]
    misses = [identity - t.astype(F32) - mm2l(lower, t) for lower, t in zip(lowers, rounded)]
    return [t.astype(F32) + dot(t, miss.astype(BF16)) for t, miss in zip(rounded, misses)]


def kernel(
    q_in, k_in, v_in, gate_in, ws_in, ld_in, w_in, gain_ref, out_ref,
    qbuf, kbuf, vbuf, gate, gating, ws, ld, wbuf, gb_send, gb_recv,
    kc, fs, tinv, ew, mc, ac, pre, m_send, a_send, m_recv, a_recv,
    mpre, msuf, apre, ym_send, ya_send, ym_recv, ya_recv, h_send, h_recv, pb, o_send, o_recv,
    local_sem, send_sem, recv_sem,
):
    s = lax.axis_index("seq")
    z = lax.axis_index("head")
    y = s // LINE
    l = lax.rem(s, LINE)

    def at_head(d):
        return lax.rem(z + d, GROUPS)

    def at_line(d):
        return lax.rem(l + d, LINE)

    barrier = pltpu.get_barrier_semaphore()
    for d in range(1, GROUPS):
        pl.semaphore_signal(barrier, inc=1, device_id=(s, at_head(d)), device_id_type=MESH)
    for d in range(1, LINE):
        pl.semaphore_signal(barrier, inc=1, device_id=(y * LINE + at_line(d), z), device_id_type=MESH)
    for d in range(1, LINES):
        pl.semaphore_signal(
            barrier, inc=1, device_id=(lax.rem(y + d, LINES) * LINE + l, z), device_id_type=MESH
        )
    pl.semaphore_signal(barrier, inc=1, device_id=(lax.rem(s + SEQ - 1, SEQ), z), device_id_type=MESH)

    mine = pl.ds(pl.multiple_of(RIM + z * TOK, RIM), TOK)

    def own_columns(width):
        return pl.ds(pl.multiple_of(z * width, width), width)

    copies = [
        pltpu.make_async_copy(ws_in, ws, local_sem.at[0]),
        pltpu.make_async_copy(ld_in, ld, local_sem.at[1]),
        pltpu.make_async_copy(w_in, wbuf, local_sem.at[2]),
        pltpu.make_async_copy(k_in.at[:, own_columns(256)], kbuf.at[mine, :], local_sem.at[3]),
        pltpu.make_async_copy(v_in.at[:, own_columns(512)], vbuf.at[mine, :], local_sem.at[4]),
        pltpu.make_async_copy(q_in.at[:, own_columns(256)], qbuf.at[mine, :], local_sem.at[5]),
        pltpu.make_async_copy(gate_in, gate, local_sem.at[6]),
    ]
    for copy in copies:
        copy.start()

    rows = lax.broadcasted_iota(jnp.int32, (C, C), 0)
    cols = lax.broadcasted_iota(jnp.int32, (C, C), 1)
    eye = rows == cols
    tril = rows >= cols
    strict = rows > cols

    copies[0].wait()
    copies[1].wait()
    upto = jnp.where(rows <= cols, 1.0, 0.0)[:TOK, :TOK].astype(BF16)
    running = dot(ld[...], upto)
    both = jnp.concatenate([ws[...].astype(F32), running], axis=0)
    both = jnp.concatenate([both, both], axis=1)
    for g in range(GROUPS):
        gb_send[g] = jnp.concatenate(
            [both[HEADS * g : HEADS * g + HEADS], both[32 + HEADS * g : 32 + HEADS * g + HEADS]], axis=0
        )
    pl.semaphore_wait(barrier, GROUPS - 1 + LINE - 1 + LINES - 1 + 1)

    def to_head(kind, d, src, dst):
        return pltpu.make_async_remote_copy(
            src_ref=src,
            dst_ref=dst,
            send_sem=send_sem.at[kind, d],
            recv_sem=recv_sem.at[kind, d],
            device_id=(s, at_head(d)),
            device_id_type=MESH,
        )

    def to_seq(kind, d, target, src, dst):
        return pltpu.make_async_remote_copy(
            src_ref=src,
            dst_ref=dst,
            send_sem=send_sem.at[kind, d],
            recv_sem=recv_sem.at[kind, d],
            device_id=(target, z),
            device_id_type=MESH,
        )

    def columns_to(d, width):
        return pl.ds(pl.multiple_of(at_head(d) * width, width), width)

    order = [4, 3, 5, 2, 6, 1, 7]
    k_copies, v_copies, q_copies, g_copies = [], [], [], []
    for d in order:
        g_copies.append(to_head(0, d, gb_send.at[at_head(d)], gb_recv.at[z]))
        k_copies.append(to_head(1, d, k_in.at[:, columns_to(d, 256)], kbuf.at[mine, :]))
    for d in order:
        v_copies.append(to_head(2, d, v_in.at[:, columns_to(d, 512)], vbuf.at[mine, :]))
    for d in order:
        q_copies.append(to_head(3, d, q_in.at[:, columns_to(d, 256)], qbuf.at[mine, :]))
    for copy in g_copies + k_copies + v_copies + q_copies:
        copy.start()
    gb_recv[z] = gb_send[z]

    copies[6].wait()
    gain = jnp.concatenate([gain_ref[...]] * HEADS, axis=1)

    def gate_body(g, carry):
        here = pl.ds(pl.multiple_of(g * 512, 512), 512)
        gating[:, here] = silu(gate[:, here].astype(F32)) * gain
        return carry

    lax.fori_loop(0, GROUPS, gate_body, 0)

    following = lax.rem(s + 1, SEQ)

    def rim_copy(index, buf):
        return to_seq(4, index, following, buf.at[pl.ds(ROWS, RIM), :], buf.at[pl.ds(0, RIM), :])

    def arrived(own, others, index, buf):
        own.wait()
        for copy in others:
            copy.wait_recv()
        rim = rim_copy(index, buf)
        rim.start()
        return rim

    def rim_arrived(rim, buf):
        rim.wait_recv()

        @pl.when(s == 0)
        def _():
            buf[pl.ds(0, RIM), :] = jnp.zeros((RIM, buf.shape[1]), BF16)

    def chunk_scales(c):
        first, second = gb_recv[2 * c], gb_recv[2 * c + 1]
        lane = lax.broadcasted_iota(jnp.int32, (8, C), 1)
        sub = lax.broadcasted_iota(jnp.int32, (8, C), 0)
        carry = jnp.where(sub >= HEADS, first[:, TOK - 1 : TOK], 0.0)
        across = jnp.where(lane < TOK, first, second + carry)
        return across, across.T

    copies[2].wait()
    for copy in g_copies:
        copy.wait_recv()
    k_rim = arrived(copies[3], k_copies, 0, kbuf)
    taps_k = wbuf[:, pl.ds(pl.multiple_of(2048 + z * 256, 256), 256)].astype(F32)

    def key_body(i, carry):
        c = lax.rem(i + 1, CHUNKS)

        @pl.when(i == CHUNKS - 1)
        def _():
            rim_arrived(k_rim, kbuf)

        start = pl.multiple_of(c * C, C)
        block = pl.ds(start, C)
        keys = conv(kbuf, start, taps_k)
        kc[block, :] = keys
        across, down = chunk_scales(c)
        b_cols = [down[:, h : h + 1] for h in range(HEADS)]
        c_cols = [down[:, HEADS + h : HEADS + h + 1] for h in range(HEADS)]
        b_rows = [across[h : h + 1] for h in range(HEADS)]
        c_rows = [across[HEADS + h : HEADS + h + 1] for h in range(HEADS)]
        ends = [c_row[:, C - 1 : C] for c_row in c_rows]
        key = [keys[:, kh * D : (kh + 1) * D] for kh in range(2)]
        kk = [dot(part, part, NT) for part in key]
        diagonal = [jnp.where(eye, part, 0.0) for part in kk]
        s_cols = [lax.rsqrt(jnp.sum(part, axis=1, keepdims=True) + EPSILON) for part in diagonal]
        s_rows = [lax.rsqrt(jnp.sum(part, axis=0, keepdims=True) + EPSILON) for part in diagonal]
        lowers = []
        for h in range(HEADS):
            fade = jnp.where(tril, jnp.exp(jnp.where(tril, c_cols[h] - c_rows[h], 0.0)), 0.0) * s_rows[h // 2]
            fs[h, block, :] = fade
            lowers.append(jnp.where(strict, kk[h // 2] * fade * (s_cols[h // 2] * b_cols[h]), 0.0))
        ts = [t * b_row for t, b_row in zip(unit_inverses(lowers, rows, cols), b_rows)]
        for h in range(HEADS):
            tinv[h, block, :] = ts[h]
        erases = [mm2l(ts[h] * (s_rows[h // 2] * jnp.exp(c_rows[h])), key[h // 2]) for h in range(HEADS)]
        for h in range(HEADS):
            ew[h, block, pl.ds(0, D)] = erases[h]
        takens = [
            mm2r(key[h // 2], erases[h] * (s_cols[h // 2] * jnp.exp(ends[h] - c_cols[h])), TN)
            for h in range(HEADS)
        ]
        for h in range(HEADS):
            mc[h, c] = jnp.where(eye, jnp.exp(ends[h]), 0.0) - takens[h]
        return carry

    lax.fori_loop(0, CHUNKS, key_body, 0)

    identity = jnp.where(eye, 1.0, 0.0)
    left, right = pl.ds(0, D), pl.ds(D, D)
    for h in range(HEADS):
        pre[h, 0, :, left] = identity
        pre[h, 0, :, right] = jnp.zeros((D, D), F32)
    runnings = [mc[h, 0] for h in range(HEADS)]
    for c in range(1, CHUNKS):
        for h in range(HEADS):
            pre[h, c, :, left] = runnings[h]
        runnings = [mm3(mc[h, c], runnings[h]) for h in range(HEADS)]
    for h in range(HEADS):
        m_send[h] = runnings[h]

    def unit_head(u):
        return u // 2

    def unit_half(u):
        return pl.ds(pl.multiple_of(lax.rem(u, 2) * 64, 64), 64)

    m_copies, a_copies, h_copies = [], [], []
    for d in range(1, LINE):
        u = at_line(d)
        target = y * LINE + u
        m_copies.append(to_seq(5, d, target, m_send.at[unit_head(u)], m_recv.at[l]))
        a_copies.append(to_seq(6, d, target, a_send.at[unit_head(u), unit_half(u), :], a_recv.at[l]))
        h_copies.append(to_seq(7, d, target, h_send.at[u], h_recv.at[l]))
    for copy in m_copies:
        copy.start()
    m_recv[l] = m_send[unit_head(l)]

    v_rim = arrived(copies[4], v_copies, 1, vbuf)
    taps_v = wbuf[:, pl.ds(pl.multiple_of(4096 + z * 512, 512), 512)].astype(F32)

    def value_body(i, carry):
        c = lax.rem(i + 1, CHUNKS)

        @pl.when(i == CHUNKS - 1)
        def _():
            rim_arrived(v_rim, vbuf)

        start = pl.multiple_of(c * C, C)
        block = pl.ds(start, C)
        values = conv(vbuf, start, taps_v)
        across, down = chunk_scales(c)
        for kh in range(2):
            key = kc[block, pl.ds(kh * D, D)]
            key32 = key.astype(F32)
            s_col = lax.rsqrt(jnp.sum(key32 * key32, axis=1, keepdims=True) + EPSILON)
            for j in range(2):
                h = kh * 2 + j
                c_col = down[:, HEADS + h : HEADS + h + 1]
                end = across[HEADS + h : HEADS + h + 1, C - 1 : C]
                write = mm2l(tinv[h, block, :], values[:, h * D : (h + 1) * D])
                ew[h, block, pl.ds(D, D)] = write
                ac[h, c] = mm2r(key, write * (s_col * jnp.exp(end - c_col)), TN)
        return carry

    lax.fori_loop(0, CHUNKS, value_body, 0)
    runnings = [ac[h, 0] for h in range(HEADS)]
    for c in range(1, CHUNKS):
        for h in range(HEADS):
            pre[h, c, :, right] = runnings[h]
        runnings = [mm3(mc[h, c], runnings[h]) + ac[h, c] for h in range(HEADS)]
    for h in range(HEADS):
        a_send[h] = runnings[h].T
    for copy in a_copies:
        copy.start()
    a_recv[l] = a_send[unit_head(l), unit_half(l), :]

    for copy in m_copies:
        copy.wait_recv()
    running, later = m_recv[0], m_recv[LINE - 1]
    for i in range(1, LINE):
        mpre[i] = running
        running = mm3(m_recv[i], running)
        msuf[LINE - 1 - i] = later
        if i < LINE - 1:
            later = mm3(later, m_recv[LINE - 1 - i])
    ym_send[...] = running
    ym_copies, ya_copies = [], []
    for d in range(1, LINES):
        target = lax.rem(y + d, LINES) * LINE + l
        ym_copies.append(to_seq(8, d, target, ym_send, ym_recv.at[d - 1]))
        ya_copies.append(to_seq(9, d, target, ya_send, ya_recv.at[d - 1]))
    for copy in ym_copies:
        copy.start()
    for copy in a_copies:
        copy.wait_recv()
    total = a_recv[LINE - 1]
    for i in range(LINE - 1):
        total = total + mm3(a_recv[i], msuf[i], NT)
    ya_send[...] = total
    for copy in ya_copies:
        copy.start()

    running = a_recv[0]
    for i in range(1, LINE):
        apre[i] = running
        if i < LINE - 1:
            running = mm3(running, m_recv[i], NT) + a_recv[i]

    for copy in ym_copies:
        copy.wait_recv()
    across_two = mm3(ym_recv[0], ym_recv[1])
    for copy in ya_copies:
        copy.wait_recv()
    entering = jnp.where(y >= 1, ya_recv[0], 0.0)
    entering = entering + jnp.where(y >= 2, mm3(ya_recv[1], ym_recv[0], NT), 0.0)
    entering = entering + jnp.where(y >= 3, mm3(ya_recv[2], across_two, NT), 0.0)
    h_send[0] = entering
    for i in range(1, LINE):
        h_send[i] = mm3(entering, mpre[i], NT) + apre[i]
    for copy in h_copies:
        copy.start()
    h_recv[l] = h_send[l]

    q_rim = arrived(copies[5], q_copies, 2, qbuf)
    taps_q = wbuf[:, pl.ds(pl.multiple_of(z * 256, 256), 256)].astype(F32)

    def query_body(i, carry):
        c = lax.rem(i + 1, CHUNKS)

        @pl.when(i == CHUNKS - 1)
        def _():
            rim_arrived(q_rim, qbuf)

        start = pl.multiple_of(c * C, C)
        block = pl.ds(start, C)
        queries = conv(qbuf, start, taps_q)
        across, down = chunk_scales(c)
        for kh in range(2):
            key = kc[block, pl.ds(kh * D, D)]
            query = queries[:, kh * D : (kh + 1) * D]
            query32 = query.astype(F32)
            s_col = lax.rsqrt(jnp.sum(query32 * query32, axis=1, keepdims=True) + EPSILON) * (D**-0.5)
            qk = dot(query, key, NT) * s_col
            for j in range(2):
                h = kh * 2 + j
                c_col = down[:, HEADS + h : HEADS + h + 1]
                inner = mm3(qk * fs[h, block, :], ew[h, block, :])
                reads = query32 * (s_col * jnp.exp(c_col)) - inner[:, :D]
                outer = mm3(reads, pre[h, c])
                pb[h, block, left] = outer[:, :D]
                pb[h, block, right] = outer[:, D:] + inner[:, D:]
        return carry

    lax.fori_loop(0, CHUNKS, query_body, 0)

    for copy in h_copies:
        copy.wait_recv()
    o_copies = []
    for d in range(1, GROUPS):
        o_copies.append(to_head(10, d, o_send.at[at_head(d)], o_recv.at[z]))

    def out_rows(t):
        block = pl.ds(pl.multiple_of(t * TOK, TOK), TOK)
        for h in range(HEADS):
            state = jnp.concatenate([h_recv[2 * h], h_recv[2 * h + 1]], axis=0)
            o = mm3(pb[h, block, left], state, NT) + pb[h, block, right]
            o_send[t, :, pl.ds(h * D, D)] = o.astype(BF16)

    for copy, d in zip(o_copies, range(1, GROUPS)):
        out_rows(at_head(d))
        copy.start()
    out_rows(z)
    o_recv[z] = o_send[z]

    def norm(g):
        for h in range(HEADS):
            a = o_recv[g, :, pl.ds(h * D, D)].astype(F32)
            a = a * lax.rsqrt(jnp.mean(a * a, axis=1, keepdims=True) + EPSILON)
            here = pl.ds(pl.multiple_of(g * 512 + h * D, D), D)
            out_ref[:, here] = (a * gating[:, here]).astype(BF16)

    norm(z)
    for d in (1, 7, 2, 6, 3, 5, 4):
        o_copies[d - 1].wait_recv()
        norm(lax.rem(z + GROUPS - d, GROUPS))

    for copy in g_copies + k_copies + v_copies + q_copies + [k_rim, v_rim, q_rim]:
        copy.wait_send()
    for copy in m_copies + a_copies + h_copies + ym_copies + ya_copies + o_copies:
        copy.wait_send()


def local(query_in, key_in, value_in, gate_in, write_strength, log_decay, conv_weight, norm_gain):
    anywhere = pl.BlockSpec(memory_space=pl.ANY)
    vmem = pl.BlockSpec(memory_space=pltpu.VMEM)
    return pl.pallas_call(
        kernel,
        out_shape=jax.ShapeDtypeStruct((TOK, 4096), BF16),
        in_specs=[anywhere] * 7 + [vmem],
        out_specs=vmem,
        scratch_shapes=[
            pltpu.VMEM((RIM + ROWS, 256), BF16),
            pltpu.VMEM((RIM + ROWS, 256), BF16),
            pltpu.VMEM((RIM + ROWS, 512), BF16),
            pltpu.VMEM((TOK, 4096), BF16),
            pltpu.VMEM((TOK, 4096), F32),
            pltpu.VMEM((32, TOK), BF16),
            pltpu.VMEM((32, TOK), BF16),
            pltpu.VMEM((4, 8192), BF16),
            pltpu.VMEM((GROUPS, 8, C), F32),
            pltpu.VMEM((GROUPS, 8, C), F32),
            pltpu.VMEM((ROWS, 256), BF16),
            pltpu.VMEM((HEADS, ROWS, C), F32),
            pltpu.VMEM((HEADS, ROWS, C), F32),
            pltpu.VMEM((HEADS, ROWS, 2 * D), F32),
            pltpu.VMEM((HEADS, CHUNKS, D, D), F32),
            pltpu.VMEM((HEADS, CHUNKS, D, D), F32),
            pltpu.VMEM((HEADS, CHUNKS, D, 2 * D), F32),
            pltpu.VMEM((HEADS, D, D), F32),
            pltpu.VMEM((HEADS, D, D), F32),
            pltpu.VMEM((LINE, D, D), F32),
            pltpu.VMEM((LINE, 64, D), F32),
            pltpu.VMEM((LINE, D, D), F32),
            pltpu.VMEM((LINE, D, D), F32),
            pltpu.VMEM((LINE, 64, D), F32),
            pltpu.VMEM((D, D), F32),
            pltpu.VMEM((64, D), F32),
            pltpu.VMEM((LINES - 1, D, D), F32),
            pltpu.VMEM((LINES - 1, 64, D), F32),
            pltpu.VMEM((LINE, 64, D), F32),
            pltpu.VMEM((LINE, 64, D), F32),
            pltpu.VMEM((HEADS, ROWS, 2 * D), F32),
            pltpu.VMEM((GROUPS, TOK, 512), BF16),
            pltpu.VMEM((GROUPS, TOK, 512), BF16),
            pltpu.SemaphoreType.DMA((7,)),
            pltpu.SemaphoreType.DMA((11, 8)),
            pltpu.SemaphoreType.DMA((11, 8)),
        ],
        compiler_params=pltpu.CompilerParams(
            collective_id=0, has_side_effects=True, vmem_limit_bytes=60 * 1024 * 1024
        ),
    )(
        query_in, key_in, value_in, gate_in, write_strength.T, log_decay.T, conv_weight, norm_gain.reshape(1, D)
    )


def solution(mesh):
    rows = P(("seq", "head"), None)
    return jax.shard_map(
        local,
        mesh=mesh,
        in_specs=(rows, rows, rows, rows, rows, rows, P(), P()),
        out_specs=rows,
        check_vma=False,
    )
```

```python
import functools

import jax
import jax.numpy as jnp
from jax import lax
from jax.experimental import pallas as pl
from jax.experimental.pallas import tpu as pltpu
from jax.sharding import PartitionSpec as P

MESH = pl.DeviceIdType.MESH
F32 = jnp.float32
BF16 = jnp.bfloat16
EPSILON = 1e-06

GROUPS = 8
TOK = 64
LINE = 8
LINES = 4
SEQ = LINE * LINES
HEADS = 4
D = 128
C = 128
ROWS = TOK * GROUPS
CHUNKS = ROWS // C
RIM = 16
PAIR = 2

NN = (((1,), (0,)), ((), ()))
NT = (((1,), (1,)), ((), ()))
TN = (((0,), (0,)), ((), ()))


def dot(a, b, dims=NN):
    return lax.dot_general(a, b, dims, preferred_element_type=F32)


def split(x):
    high = x.astype(BF16)
    return high, (x - high.astype(F32)).astype(BF16)


def beside(b1, b2, dims):
    return jnp.concatenate([b1, b2], axis=0 if dims == NT else 1)


def mm2l(a, b, dims=NN):
    a1, a2 = split(a)
    axis = 1 if dims == NT else 0
    return dot(jnp.concatenate([a1, a2], axis=1), jnp.concatenate([b, b], axis=axis), dims)


def mm2r(a, b, dims=NN):
    b1, b2 = split(b)
    both = dot(a, beside(b1, b2, dims), dims)
    half = both.shape[1] // 2
    return both[:, :half] + both[:, half:]


def mm3(a, b, dims=NN):
    a1, a2 = split(a)
    b1, b2 = split(b)
    if b.shape[0 if dims == NT else 1] > D:
        axis = 1 if dims == NT else 0
        main = dot(jnp.concatenate([a1, a2], axis=1), jnp.concatenate([b1, b1], axis=axis), dims)
        return main + dot(a1, b2, dims)
    both = dot(a1, beside(b1, b2, dims), dims)
    half = both.shape[1] // 2
    return both[:, :half] + both[:, half:] + dot(a2, b1, dims)


def pack_map(m, f_row, eye):
    sub = lax.broadcasted_iota(jnp.int32, (RIM, D), 0)
    f1 = f_row.astype(BF16).astype(F32)
    f2 = (f_row - f1).astype(BF16).astype(F32)
    pieces = jnp.where(sub == 0, f1, jnp.where(sub == 1, f2, jnp.where(sub == 2, f_row - f1 - f2, 0.0)))
    return jnp.concatenate([m - jnp.where(eye, f_row, 0.0), pieces], axis=0).astype(BF16)


def unpack_map(packed, eye):
    f_row = jnp.sum(packed[D:].astype(F32), axis=0, keepdims=True)
    return packed[:D].astype(F32) + jnp.where(eye, f_row, 0.0), f_row


def silu(x):
    return x / (1.0 + jnp.exp(-x))


def conv(buf, start, taps):
    x = buf[pl.ds(start, C + RIM), :].astype(F32)
    total = x[RIM - 3 : RIM - 3 + C] * taps[0:1]
    for j in range(1, 4):
        total = total + x[RIM - 3 + j : RIM - 3 + j + C] * taps[j : j + 1]
    return silu(total).astype(BF16)


def odd_blocks(x, size):
    return jnp.concatenate([x[i : i + size] for i in range(size, C, 2 * size)], axis=0)


def to_odd_blocks(x, size):
    zero = jnp.zeros((size, x.shape[1]), x.dtype)
    parts = []
    for i in range(0, C // 2, size):
        parts += [zero, x[i : i + size]]
    return jnp.concatenate(parts, axis=0)


def unit_inverses(lowers, rows, cols):
    identity = jnp.where(rows == cols, 1.0, 0.0)
    base = (rows // 8) * 8
    ts = [identity.reshape(C // 8, 8, C)] * len(lowers)
    for j in range(7):
        picked = cols == base + j
        for n, lower in enumerate(lowers):
            factor = jnp.sum(jnp.where(picked, lower, 0.0), axis=1, keepdims=True).reshape(C // 8, 8, 1)
            ts[n] = ts[n] - factor * ts[n][:, j : j + 1, :]
    ts = [t.reshape(C, C) for t in ts]
    size = 8
    while size < C:
        below = odd_blocks(cols // size, size) == odd_blocks(rows // size, size) - 1
        parts = [jnp.where(below, odd_blocks(lower, size), 0.0).astype(BF16) for lower in lowers]
        firsts = [dot(part, t.astype(BF16)) for part, t in zip(parts, ts)]
        seconds = [
            dot(odd_blocks(t, size).astype(BF16), to_odd_blocks(first, size).astype(BF16))
            for t, first in zip(ts, firsts)
        ]
        ts = [t - to_odd_blocks(second, size) for t, second in zip(ts, seconds)]
        size *= 2
    rounded = [t.astype(BF16) for t in ts]
    misses = [identity - t.astype(F32) - mm2l(lower, t) for lower, t in zip(lowers, rounded)]
    return [t.astype(F32) + dot(t, miss.astype(BF16)) for t, miss in zip(rounded, misses)]


def kernel(
    q_in, k_in, v_in, gate_in, ws_in, ld_in, w_in, gain_ref, out_ref,
    qbuf, kbuf, vbuf, gate, gating, ws, ld, wbuf, gb_send, gb_recv,
    kc, fs, tinv, ew, mc, ac, pre, m_send, a_send, m_recv, maps, a_recv,
    mpre, msuf, mpair, apre, ym_send, ya_send, ym_recv, ya_recv, h_send, h_recv, pb, o_send, o_recv,
    local_sem, send_sem, recv_sem, rim_sem,
):
    s = lax.axis_index("seq")
    z = lax.axis_index("head")
    y = s // LINE
    l = lax.rem(s, LINE)

    def at_head(d):
        return lax.rem(z + d, GROUPS)

    def at_line(d):
        return lax.rem(l + d, LINE)

    barrier = pltpu.get_barrier_semaphore()
    for d in range(1, GROUPS):
        pl.semaphore_signal(barrier, inc=1, device_id=(s, at_head(d)), device_id_type=MESH)
    for d in range(1, LINE):
        pl.semaphore_signal(barrier, inc=1, device_id=(y * LINE + at_line(d), z), device_id_type=MESH)
    for d in range(1, LINES):
        pl.semaphore_signal(
            barrier, inc=1, device_id=(lax.rem(y + d, LINES) * LINE + l, z), device_id_type=MESH
        )
    pl.semaphore_signal(
        barrier, inc=1, device_id=(lax.rem(s + SEQ - 1, SEQ), GROUPS - 1), device_id_type=MESH
    )

    mine = pl.ds(pl.multiple_of(RIM + z * TOK, RIM), TOK)

    def own_columns(width):
        return pl.ds(pl.multiple_of(z * width, width), width)

    copies = [
        pltpu.make_async_copy(ws_in, ws, local_sem.at[0]),
        pltpu.make_async_copy(ld_in, ld, local_sem.at[1]),
        pltpu.make_async_copy(w_in, wbuf, local_sem.at[2]),
        pltpu.make_async_copy(k_in.at[:, own_columns(256)], kbuf.at[mine, :], local_sem.at[3]),
        pltpu.make_async_copy(v_in.at[:, own_columns(512)], vbuf.at[mine, :], local_sem.at[4]),
        pltpu.make_async_copy(q_in.at[:, own_columns(256)], qbuf.at[mine, :], local_sem.at[5]),
        pltpu.make_async_copy(gate_in, gate, local_sem.at[6]),
    ]
    for copy in copies:
        copy.start()

    rows = lax.broadcasted_iota(jnp.int32, (C, C), 0)
    cols = lax.broadcasted_iota(jnp.int32, (C, C), 1)
    eye = rows == cols
    tril = rows >= cols
    strict = rows > cols

    partners = GROUPS - 1 + LINE - 1 + LINES - 1

    @pl.when(z < GROUPS - 1)
    def _():
        pl.semaphore_wait(barrier, partners)

    @pl.when(z == GROUPS - 1)
    def _():
        pl.semaphore_wait(barrier, partners + GROUPS)

    def to_head(kind, d, src, dst):
        return pltpu.make_async_remote_copy(
            src_ref=src,
            dst_ref=dst,
            send_sem=send_sem.at[kind, d],
            recv_sem=recv_sem.at[kind, d],
            device_id=(s, at_head(d)),
            device_id_type=MESH,
        )

    def to_seq(kind, d, target, src, dst):
        return pltpu.make_async_remote_copy(
            src_ref=src,
            dst_ref=dst,
            send_sem=send_sem.at[kind, d],
            recv_sem=recv_sem.at[kind, d],
            device_id=(target, z),
            device_id_type=MESH,
        )

    def columns_to(d, width):
        return pl.ds(pl.multiple_of(at_head(d) * width, width), width)

    near = [1, 7, 2, 6, 3, 5, 4]
    k_copies = [to_head(1, d, k_in.at[:, columns_to(d, 256)], kbuf.at[mine, :]) for d in near]
    v_copies = [to_head(2, d, v_in.at[:, columns_to(d, 512)], vbuf.at[mine, :]) for d in near]
    q_copies = [to_head(3, d, q_in.at[:, columns_to(d, 256)], qbuf.at[mine, :]) for d in near]
    g_copies = [to_head(0, d, gb_send.at[at_head(d)], gb_recv.at[z]) for d in near]
    following = lax.rem(s + 1, SEQ)

    def rim_copies(index, source, buf, width):
        return [
            pltpu.make_async_remote_copy(
                src_ref=source.at[pl.ds(TOK - RIM, RIM), pl.ds(g * width, width)],
                dst_ref=buf.at[pl.ds(0, RIM), :],
                send_sem=rim_sem.at[index, g],
                recv_sem=recv_sem.at[4, index],
                device_id=(following, g),
                device_id_type=MESH,
            )
            for g in range(GROUPS)
        ]

    k_rims = rim_copies(0, k_in, kbuf, 256)
    v_rims = rim_copies(1, v_in, vbuf, 512)
    q_rims = rim_copies(2, q_in, qbuf, 256)

    def start_rims(rims):
        @pl.when(z == GROUPS - 1)
        def _():
            for rim in rims:
                rim.start()

    start_rims(k_rims)
    for copy in k_copies:
        copy.start()

    copies[0].wait()
    copies[1].wait()
    upto = jnp.where(rows <= cols, 1.0, 0.0)[:TOK, :TOK].astype(BF16)
    sums = dot(ld[...], upto)
    both = jnp.concatenate([ws[...].astype(F32), sums], axis=0)
    both = jnp.concatenate([both, both], axis=1)
    for g in range(GROUPS):
        gb_send[g] = jnp.concatenate(
            [both[HEADS * g : HEADS * g + HEADS], both[32 + HEADS * g : 32 + HEADS * g + HEADS]], axis=0
        )
    start_rims(v_rims)
    for copy in g_copies + v_copies:
        copy.start()
    gb_recv[z] = gb_send[z]

    copies[6].wait()
    gain = jnp.concatenate([gain_ref[...]] * HEADS, axis=1)

    def gate_body(g, carry):
        here = pl.ds(pl.multiple_of(g * 512, 512), 512)
        gating[:, here] = silu(gate[:, here].astype(F32)) * gain
        return carry

    lax.fori_loop(0, GROUPS, gate_body, 0)

    def arrived(own, others):
        own.wait()
        for copy in others:
            copy.wait_recv()

    def rim_arrived(rim, buf):
        rim.wait_recv()

        @pl.when(s == 0)
        def _():
            buf[pl.ds(0, RIM), :] = jnp.zeros((RIM, buf.shape[1]), BF16)

    def chunk_scales(c):
        first, second = gb_recv[2 * c], gb_recv[2 * c + 1]
        lane = lax.broadcasted_iota(jnp.int32, (8, C), 1)
        sub = lax.broadcasted_iota(jnp.int32, (8, C), 0)
        carry = jnp.where(sub >= HEADS, first[:, TOK - 1 : TOK], 0.0)
        across = jnp.where(lane < TOK, first, second + carry)
        return across, across.T

    copies[2].wait()
    for copy in g_copies:
        copy.wait_recv()
    arrived(copies[3], k_copies)
    taps_k = wbuf[:, pl.ds(pl.multiple_of(2048 + z * 256, 256), 256)].astype(F32)

    def key_body(i, carry):
        @pl.when(i == CHUNKS // PAIR - 1)
        def _():
            rim_arrived(k_rims[0], kbuf)

        units = []
        for n in range(PAIR):
            c = lax.rem(i * PAIR + PAIR + n, CHUNKS)
            start = pl.multiple_of(c * C, C)
            keys = conv(kbuf, start, taps_k)
            kc[pl.ds(start, C), :] = keys
            across, down = chunk_scales(c)
            for kh in range(2):
                key = keys[:, kh * D : (kh + 1) * D]
                kk = dot(key, key, NT)
                diagonal = jnp.where(eye, kk, 0.0)
                s_col = lax.rsqrt(jnp.sum(diagonal, axis=1, keepdims=True) + EPSILON)
                s_row = lax.rsqrt(jnp.sum(diagonal, axis=0, keepdims=True) + EPSILON)
                for j in range(2):
                    h = kh * 2 + j
                    b_col, c_col = down[:, h : h + 1], down[:, HEADS + h : HEADS + h + 1]
                    b_row, c_row = across[h : h + 1], across[HEADS + h : HEADS + h + 1]
                    end = c_row[:, C - 1 : C]
                    fade = jnp.where(tril, jnp.exp(jnp.where(tril, c_col - c_row, 0.0)), 0.0) * s_row
                    fs[h, pl.ds(start, C), :] = fade
                    lower = jnp.where(strict, kk * fade * (s_col * b_col), 0.0)
                    units.append((
                        h, c, pl.ds(start, C), key, lower, b_row, s_row * jnp.exp(c_row),
                        s_col * jnp.exp(end - c_col), jnp.exp(end),
                    ))
        ts = unit_inverses([unit[4] for unit in units], rows, cols)
        ts = [t * unit[5] for t, unit in zip(ts, units)]
        for t, unit in zip(ts, units):
            tinv[unit[0], unit[2], :] = t
        erases = [mm2l(t * unit[6], unit[3]) for t, unit in zip(ts, units)]
        for erase, unit in zip(erases, units):
            ew[unit[0], unit[2], pl.ds(0, D)] = erase
        takens = [mm2r(unit[3], erase * unit[7], TN) for erase, unit in zip(erases, units)]
        for taken, unit in zip(takens, units):
            mc[unit[0], unit[1]] = jnp.where(eye, unit[8], 0.0) - taken
        return carry

    lax.fori_loop(0, CHUNKS // PAIR, key_body, 0)

    identity = jnp.where(eye, 1.0, 0.0)
    left, right = pl.ds(0, D), pl.ds(D, D)
    for h in range(HEADS):
        pre[h, 0, :, left] = identity
        pre[h, 0, :, right] = jnp.zeros((D, D), F32)
    runnings = [mc[h, 0] for h in range(HEADS)]
    for c in range(1, CHUNKS):
        for h in range(HEADS):
            pre[h, c, :, left] = runnings[h]
        runnings = [mm3(mc[h, c], runnings[h]) for h in range(HEADS)]
    for h in range(HEADS):
        decay = gb_recv[0, HEADS + h : HEADS + h + 1, TOK - 1 : TOK]
        for g in range(1, GROUPS):
            decay = decay + gb_recv[g, HEADS + h : HEADS + h + 1, TOK - 1 : TOK]
        m_send[h] = pack_map(runnings[h], jnp.broadcast_to(jnp.exp(decay), (1, D)), eye)

    def unit_head(u):
        return u // 2

    def unit_half(u):
        return pl.ds(pl.multiple_of(lax.rem(u, 2) * 64, 64), 64)

    m_copies, a_copies, h_copies = [], [], []
    for d in range(1, LINE):
        u = at_line(d)
        target = y * LINE + u
        m_copies.append(to_seq(5, d, target, m_send.at[unit_head(u)], m_recv.at[l]))
        a_copies.append(to_seq(6, d, target, a_send.at[unit_head(u), unit_half(u), :], a_recv.at[l]))
        h_copies.append(to_seq(7, d, target, h_send.at[u], h_recv.at[l]))
    start_rims(q_rims)
    for copy in m_copies + q_copies:
        copy.start()
    m_recv[l] = m_send[unit_head(l)]

    arrived(copies[4], v_copies)
    taps_v = wbuf[:, pl.ds(pl.multiple_of(4096 + z * 512, 512), 512)].astype(F32)

    def value_body(i, carry):
        @pl.when(i == CHUNKS // PAIR - 1)
        def _():
            rim_arrived(v_rims[0], vbuf)

        for n in range(PAIR):
            c = lax.rem(i * PAIR + PAIR + n, CHUNKS)
            start = pl.multiple_of(c * C, C)
            block = pl.ds(start, C)
            values = conv(vbuf, start, taps_v)
            across, down = chunk_scales(c)
            for kh in range(2):
                key = kc[block, pl.ds(kh * D, D)]
                key32 = key.astype(F32)
                s_col = lax.rsqrt(jnp.sum(key32 * key32, axis=1, keepdims=True) + EPSILON)
                for j in range(2):
                    h = kh * 2 + j
                    c_col = down[:, HEADS + h : HEADS + h + 1]
                    end = across[HEADS + h : HEADS + h + 1, C - 1 : C]
                    write = mm2l(tinv[h, block, :], values[:, h * D : (h + 1) * D])
                    ew[h, block, pl.ds(D, D)] = write
                    ac[h, c] = mm2r(key, write * (s_col * jnp.exp(end - c_col)), TN)
        return carry

    lax.fori_loop(0, CHUNKS // PAIR, value_body, 0)
    runnings = [ac[h, 0] for h in range(HEADS)]
    for c in range(1, CHUNKS):
        for h in range(HEADS):
            pre[h, c, :, right] = runnings[h]
        runnings = [mm3(mc[h, c], runnings[h]) + ac[h, c] for h in range(HEADS)]
    for h in range(HEADS):
        a_send[h] = runnings[h].T.astype(BF16)
    for copy in a_copies:
        copy.start()
    a_recv[l] = a_send[unit_head(l), unit_half(l), :]

    for copy in m_copies:
        copy.wait_recv()
    m, f_total = [], None
    for i in range(LINE):
        unpacked, f_row = unpack_map(m_recv[i], eye)
        maps[i] = unpacked
        m.append(unpacked)
        f_total = f_row if f_total is None else f_total * f_row
    m01, m23, m45, m67 = mm3(m[1], m[0]), mm3(m[3], m[2]), mm3(m[5], m[4]), mm3(m[7], m[6])
    m03, m47 = mm3(m23, m01), mm3(m67, m45)
    m12, m46 = mm3(m23, m[1]), mm3(m[6], m45)
    ym_send[...] = pack_map(mm3(m47, m03), f_total, eye)
    mpre[1], mpre[2], mpre[3], mpre[4] = m[0], m01, mm3(m[2], m01), m03
    mpre[5], mpre[6], mpre[7] = mm3(m[4], m03), mm3(m45, m03), mm3(m46, m03)
    msuf[6], msuf[5], msuf[4], msuf[3] = m[7], m67, mm3(m67, m[5]), m47
    msuf[2], msuf[1], msuf[0] = mm3(m47, m[3]), mm3(m47, m23), mm3(m47, m12)
    mpair[0], mpair[1] = m23, m45
    ym_copies, ya_copies = [], []
    for d in range(1, LINES):
        target = lax.rem(y + d, LINES) * LINE + l
        ym_copies.append(to_seq(8, d, target, ym_send, ym_recv.at[d - 1]))
        ya_copies.append(to_seq(9, d, target, ya_send, ya_recv.at[d - 1]))

    def start_later(across):
        for d in range(1, LINES):

            @pl.when(y + d < LINES)
            def _(d=d):
                across[d - 1].start()

    def wait_earlier(across):
        for d in range(1, LINES):

            @pl.when(y >= d)
            def _(d=d):
                across[d - 1].wait_recv()

    start_later(ym_copies)
    for copy in a_copies:
        copy.wait_recv()
    adds = [a_recv[i] for i in range(LINE)]
    total = adds[LINE - 1].astype(F32)
    for i in range(LINE - 1):
        total = total + mm2r(adds[i], msuf[i], NT)
    ya_send[...] = total
    start_later(ya_copies)

    apre[1] = adds[0].astype(F32)
    apre[2] = mm2r(adds[0], maps[1], NT) + adds[1].astype(F32)
    apre[3] = mm3(apre[2], maps[2], NT) + adds[2].astype(F32)
    apre[4] = mm3(apre[2], mpair[0], NT) + (mm2r(adds[2], maps[3], NT) + adds[3].astype(F32))
    apre[5] = mm3(apre[4], maps[4], NT) + adds[4].astype(F32)
    apre[6] = mm3(apre[4], mpair[1], NT) + (mm2r(adds[4], maps[5], NT) + adds[5].astype(F32))
    apre[7] = mm3(apre[6], maps[6], NT) + adds[6].astype(F32)

    wait_earlier(ym_copies)
    line_one = jnp.where(y >= 1, unpack_map(ym_recv[0], eye)[0], 0.0)
    line_two = jnp.where(y >= 2, mm3(line_one, unpack_map(ym_recv[1], eye)[0]), 0.0)
    wait_earlier(ya_copies)
    entering = jnp.where(y >= 1, ya_recv[0], 0.0)
    entering = entering + jnp.where(y >= 2, mm3(ya_recv[1], line_one, NT), 0.0)
    entering = entering + jnp.where(y >= 3, mm3(ya_recv[2], line_two, NT), 0.0)
    h_send[0] = entering.astype(BF16)
    for i in range(1, LINE):
        h_send[i] = (mm3(entering, mpre[i], NT) + apre[i]).astype(BF16)
    for copy in h_copies:
        copy.start()
    h_recv[l] = h_send[l]

    arrived(copies[5], q_copies)
    taps_q = wbuf[:, pl.ds(pl.multiple_of(z * 256, 256), 256)].astype(F32)

    def query_body(i, carry):
        c = lax.rem(i + 1, CHUNKS)

        @pl.when(i == CHUNKS - 1)
        def _():
            rim_arrived(q_rims[0], qbuf)

        start = pl.multiple_of(c * C, C)
        block = pl.ds(start, C)
        queries = conv(qbuf, start, taps_q)
        across, down = chunk_scales(c)
        for kh in range(2):
            key = kc[block, pl.ds(kh * D, D)]
            query = queries[:, kh * D : (kh + 1) * D]
            query32 = query.astype(F32)
            s_col = lax.rsqrt(jnp.sum(query32 * query32, axis=1, keepdims=True) + EPSILON) * (D**-0.5)
            qk = dot(query, key, NT) * s_col
            for j in range(2):
                h = kh * 2 + j
                c_col = down[:, HEADS + h : HEADS + h + 1]
                inner = mm3(qk * fs[h, block, :], ew[h, block, :])
                reads = query32 * (s_col * jnp.exp(c_col)) - inner[:, :D]
                outer = mm3(reads, pre[h, c])
                pb[h, block, left] = outer[:, :D]
                pb[h, block, right] = outer[:, D:] + inner[:, D:]
        return carry

    lax.fori_loop(0, CHUNKS, query_body, 0)

    for copy in h_copies:
        copy.wait_recv()
    far = [4, 3, 5, 2, 6, 1, 7]
    o_copies = [to_head(10, d, o_send.at[at_head(d)], o_recv.at[z]) for d in far]

    def out_rows(t):
        block = pl.ds(pl.multiple_of(t * TOK, TOK), TOK)
        for h in range(HEADS):
            state = jnp.concatenate([h_recv[2 * h], h_recv[2 * h + 1]], axis=0)
            o = mm2l(pb[h, block, left], state, NT) + pb[h, block, right]
            o_send[t, :, pl.ds(h * D, D)] = o.astype(BF16)

    for copy, d in zip(o_copies, far):
        out_rows(at_head(d))
        copy.start()
    out_rows(z)
    o_recv[z] = o_send[z]

    def norm(g):
        for h in range(HEADS):
            a = o_recv[g, :, pl.ds(h * D, D)].astype(F32)
            a = a * lax.rsqrt(jnp.mean(a * a, axis=1, keepdims=True) + EPSILON)
            here = pl.ds(pl.multiple_of(g * 512 + h * D, D), D)
            out_ref[:, here] = (a * gating[:, here]).astype(BF16)

    norm(z)
    for copy, d in zip(o_copies, far):
        copy.wait_recv()
        norm(lax.rem(z + GROUPS - d, GROUPS))

    for copy in g_copies + k_copies + v_copies + q_copies + m_copies + a_copies + h_copies + o_copies:
        copy.wait_send()

    @pl.when(z == GROUPS - 1)
    def _():
        for rim in k_rims + v_rims + q_rims:
            rim.wait_send()

    for d in range(1, LINES):

        @pl.when(y + d < LINES)
        def _(d=d):
            ym_copies[d - 1].wait_send()
            ya_copies[d - 1].wait_send()


def local(query_in, key_in, value_in, gate_in, write_strength, log_decay, conv_weight, norm_gain):
    anywhere = pl.BlockSpec(memory_space=pl.ANY)
    vmem = pl.BlockSpec(memory_space=pltpu.VMEM)
    return pl.pallas_call(
        kernel,
        out_shape=jax.ShapeDtypeStruct((TOK, 4096), BF16),
        in_specs=[anywhere] * 7 + [vmem],
        out_specs=vmem,
        scratch_shapes=[
            pltpu.VMEM((RIM + ROWS, 256), BF16),
            pltpu.VMEM((RIM + ROWS, 256), BF16),
            pltpu.VMEM((RIM + ROWS, 512), BF16),
            pltpu.VMEM((TOK, 4096), BF16),
            pltpu.VMEM((TOK, 4096), F32),
            pltpu.VMEM((32, TOK), BF16),
            pltpu.VMEM((32, TOK), BF16),
            pltpu.VMEM((4, 8192), BF16),
            pltpu.VMEM((GROUPS, 8, C), F32),
            pltpu.VMEM((GROUPS, 8, C), F32),
            pltpu.VMEM((ROWS, 256), BF16),
            pltpu.VMEM((HEADS, ROWS, C), F32),
            pltpu.VMEM((HEADS, ROWS, C), F32),
            pltpu.VMEM((HEADS, ROWS, 2 * D), F32),
            pltpu.VMEM((HEADS, CHUNKS, D, D), F32),
            pltpu.VMEM((HEADS, CHUNKS, D, D), F32),
            pltpu.VMEM((HEADS, CHUNKS, D, 2 * D), F32),
            pltpu.VMEM((HEADS, D + RIM, D), BF16),
            pltpu.VMEM((HEADS, D, D), BF16),
            pltpu.VMEM((LINE, D + RIM, D), BF16),
            pltpu.VMEM((LINE, D, D), F32),
            pltpu.VMEM((LINE, 64, D), BF16),
            pltpu.VMEM((LINE, D, D), F32),
            pltpu.VMEM((LINE, D, D), F32),
            pltpu.VMEM((2, D, D), F32),
            pltpu.VMEM((LINE, 64, D), F32),
            pltpu.VMEM((D + RIM, D), BF16),
            pltpu.VMEM((64, D), F32),
            pltpu.VMEM((LINES - 1, D + RIM, D), BF16),
            pltpu.VMEM((LINES - 1, 64, D), F32),
            pltpu.VMEM((LINE, 64, D), BF16),
            pltpu.VMEM((LINE, 64, D), BF16),
            pltpu.VMEM((HEADS, ROWS, 2 * D), F32),
            pltpu.VMEM((GROUPS, TOK, 512), BF16),
            pltpu.VMEM((GROUPS, TOK, 512), BF16),
            pltpu.SemaphoreType.DMA((7,)),
            pltpu.SemaphoreType.DMA((11, 8)),
            pltpu.SemaphoreType.DMA((11, 8)),
            pltpu.SemaphoreType.DMA((3, 8)),
        ],
        compiler_params=pltpu.CompilerParams(
            collective_id=0, has_side_effects=True, vmem_limit_bytes=60 * 1024 * 1024
        ),
    )(
        query_in, key_in, value_in, gate_in, write_strength.T, log_decay.T, conv_weight, norm_gain.reshape(1, D)
    )


def solution(mesh):
    rows = P(("seq", "head"), None)
    return jax.shard_map(
        local,
        mesh=mesh,
        in_specs=(rows, rows, rows, rows, rows, rows, P(), P()),
        out_specs=rows,
        check_vma=False,
    )
```

```python
import functools

import jax
import jax.numpy as jnp
from jax import lax
from jax.experimental import pallas as pl
from jax.experimental.pallas import tpu as pltpu
from jax.sharding import PartitionSpec as P

MESH = pl.DeviceIdType.MESH
F32 = jnp.float32
BF16 = jnp.bfloat16
EPSILON = 1e-06

GROUPS = 8
TOK = 64
LINE = 8
LINES = 4
SEQ = LINE * LINES
HEADS = 4
D = 128
C = 128
ROWS = TOK * GROUPS
CHUNKS = ROWS // C
RIM = 16
PAIR = 2

NN = (((1,), (0,)), ((), ()))
NT = (((1,), (1,)), ((), ()))
TN = (((0,), (0,)), ((), ()))


def dot(a, b, dims=NN):
    return lax.dot_general(a, b, dims, preferred_element_type=F32)


def split(x):
    high = x.astype(BF16)
    return high, (x - high.astype(F32)).astype(BF16)


def beside(b1, b2, dims):
    return jnp.concatenate([b1, b2], axis=0 if dims == NT else 1)


def mm2l(a, b, dims=NN):
    a1, a2 = split(a)
    axis = 1 if dims == NT else 0
    return dot(jnp.concatenate([a1, a2], axis=1), jnp.concatenate([b, b], axis=axis), dims)


def mm2r(a, b, dims=NN):
    b1, b2 = split(b)
    both = dot(a, beside(b1, b2, dims), dims)
    half = both.shape[1] // 2
    return both[:, :half] + both[:, half:]


def mm3(a, b, dims=NN):
    a1, a2 = split(a)
    b1, b2 = split(b)
    if b.shape[0 if dims == NT else 1] > D:
        axis = 1 if dims == NT else 0
        main = dot(jnp.concatenate([a1, a2], axis=1), jnp.concatenate([b1, b1], axis=axis), dims)
        return main + dot(a1, b2, dims)
    both = dot(a1, beside(b1, b2, dims), dims)
    half = both.shape[1] // 2
    return both[:, :half] + both[:, half:] + dot(a2, b1, dims)


def pack_map(m, f_row, eye):
    sub = lax.broadcasted_iota(jnp.int32, (RIM, D), 0)
    f1 = f_row.astype(BF16).astype(F32)
    f2 = (f_row - f1).astype(BF16).astype(F32)
    pieces = jnp.where(sub == 0, f1, jnp.where(sub == 1, f2, jnp.where(sub == 2, f_row - f1 - f2, 0.0)))
    return jnp.concatenate([m - jnp.where(eye, f_row, 0.0), pieces], axis=0).astype(BF16)


def unpack_map(packed, eye):
    f_row = jnp.sum(packed[D:].astype(F32), axis=0, keepdims=True)
    return packed[:D].astype(F32) + jnp.where(eye, f_row, 0.0), f_row


def silu(x):
    return x / (1.0 + jnp.exp(-x))


def conv(buf, start, taps):
    x = buf[pl.ds(start, C + RIM), :].astype(F32)
    total = x[RIM - 3 : RIM - 3 + C] * taps[0:1]
    for j in range(1, 4):
        total = total + x[RIM - 3 + j : RIM - 3 + j + C] * taps[j : j + 1]
    return silu(total).astype(BF16)


def odd_blocks(x, size):
    return jnp.concatenate([x[i : i + size] for i in range(size, C, 2 * size)], axis=0)


def to_odd_blocks(x, size):
    zero = jnp.zeros((size, x.shape[1]), x.dtype)
    parts = []
    for i in range(0, C // 2, size):
        parts += [zero, x[i : i + size]]
    return jnp.concatenate(parts, axis=0)


def unit_inverses(lowers, rows, cols):
    identity = jnp.where(rows == cols, 1.0, 0.0)
    base = (rows // 8) * 8
    ts = [identity.reshape(C // 8, 8, C)] * len(lowers)
    for j in range(7):
        picked = cols == base + j
        for n, lower in enumerate(lowers):
            factor = jnp.sum(jnp.where(picked, lower, 0.0), axis=1, keepdims=True).reshape(C // 8, 8, 1)
            ts[n] = ts[n] - factor * ts[n][:, j : j + 1, :]
    ts = [t.reshape(C, C) for t in ts]
    size = 8
    while size < C:
        below = odd_blocks(cols // size, size) == odd_blocks(rows // size, size) - 1
        parts = [jnp.where(below, odd_blocks(lower, size), 0.0).astype(BF16) for lower in lowers]
        firsts = [dot(part, t.astype(BF16)) for part, t in zip(parts, ts)]
        seconds = [
            dot(odd_blocks(t, size).astype(BF16), to_odd_blocks(first, size).astype(BF16))
            for t, first in zip(ts, firsts)
        ]
        ts = [t - to_odd_blocks(second, size) for t, second in zip(ts, seconds)]
        size *= 2
    rounded = [t.astype(BF16) for t in ts]
    misses = [identity - t.astype(F32) - mm2l(lower, t) for lower, t in zip(lowers, rounded)]
    return [t.astype(F32) + dot(t, miss.astype(BF16)) for t, miss in zip(rounded, misses)]


def kernel(
    q_in, k_in, v_in, gate_in, ws_in, ld_in, w_in, gain_ref, out_ref,
    qbuf, kbuf, vbuf, gate, gating, ws, ld, wbuf, gb_send, gb_recv,
    kc, fs, tinv, ew, mc, ac, pre, m_send, a_send, m_recv, maps, a_recv,
    mpre, msuf, mpair, apre, ym_send, ya_send, ym_recv, ya_recv, h_send, h_recv, pb, o_send, o_recv,
    local_sem, send_sem, recv_sem, rim_sem,
):
    s = lax.axis_index("seq")
    z = lax.axis_index("head")
    y = s // LINE
    l = lax.rem(s, LINE)

    def at_head(d):
        return lax.rem(z + d, GROUPS)

    def at_line(d):
        return lax.rem(l + d, LINE)

    barrier = pltpu.get_barrier_semaphore()
    for d in range(1, GROUPS):
        pl.semaphore_signal(barrier, inc=1, device_id=(s, at_head(d)), device_id_type=MESH)
    for d in range(1, LINE):
        pl.semaphore_signal(barrier, inc=1, device_id=(y * LINE + at_line(d), z), device_id_type=MESH)
    for d in range(1, LINES):
        pl.semaphore_signal(
            barrier, inc=1, device_id=(lax.rem(y + d, LINES) * LINE + l, z), device_id_type=MESH
        )
    pl.semaphore_signal(
        barrier, inc=1, device_id=(lax.rem(s + SEQ - 1, SEQ), GROUPS - 1), device_id_type=MESH
    )

    mine = pl.ds(pl.multiple_of(RIM + z * TOK, RIM), TOK)

    def own_columns(width):
        return pl.ds(pl.multiple_of(z * width, width), width)

    copies = [
        pltpu.make_async_copy(ws_in, ws, local_sem.at[0]),
        pltpu.make_async_copy(ld_in, ld, local_sem.at[1]),
        pltpu.make_async_copy(w_in, wbuf, local_sem.at[2]),
        pltpu.make_async_copy(k_in.at[:, own_columns(256)], kbuf.at[mine, :], local_sem.at[3]),
        pltpu.make_async_copy(v_in.at[:, own_columns(512)], vbuf.at[mine, :], local_sem.at[4]),
        pltpu.make_async_copy(q_in.at[:, own_columns(256)], qbuf.at[mine, :], local_sem.at[5]),
        pltpu.make_async_copy(gate_in, gate, local_sem.at[6]),
    ]
    for copy in copies:
        copy.start()

    rows = lax.broadcasted_iota(jnp.int32, (C, C), 0)
    cols = lax.broadcasted_iota(jnp.int32, (C, C), 1)
    eye = rows == cols
    tril = rows >= cols
    strict = rows > cols

    partners = GROUPS - 1 + LINE - 1 + LINES - 1

    @pl.when(z < GROUPS - 1)
    def _():
        pl.semaphore_wait(barrier, partners)

    @pl.when(z == GROUPS - 1)
    def _():
        pl.semaphore_wait(barrier, partners + GROUPS)

    def to_head(kind, d, src, dst):
        return pltpu.make_async_remote_copy(
            src_ref=src,
            dst_ref=dst,
            send_sem=send_sem.at[kind, d],
            recv_sem=recv_sem.at[kind, d],
            device_id=(s, at_head(d)),
            device_id_type=MESH,
        )

    def to_seq(kind, d, target, src, dst):
        return pltpu.make_async_remote_copy(
            src_ref=src,
            dst_ref=dst,
            send_sem=send_sem.at[kind, d],
            recv_sem=recv_sem.at[kind, d],
            device_id=(target, z),
            device_id_type=MESH,
        )

    def columns_to(d, width):
        return pl.ds(pl.multiple_of(at_head(d) * width, width), width)

    near = [1, 7, 2, 6, 3, 5, 4]
    k_copies = [to_head(1, d, k_in.at[:, columns_to(d, 256)], kbuf.at[mine, :]) for d in near]
    v_copies = [to_head(2, d, v_in.at[:, columns_to(d, 512)], vbuf.at[mine, :]) for d in near]
    q_copies = [to_head(3, d, q_in.at[:, columns_to(d, 256)], qbuf.at[mine, :]) for d in near]
    g_copies = [to_head(0, d, gb_send.at[at_head(d)], gb_recv.at[z]) for d in near]
    following = lax.rem(s + 1, SEQ)

    def rim_copies(index, source, buf, width):
        return [
            pltpu.make_async_remote_copy(
                src_ref=source.at[pl.ds(TOK - RIM, RIM), pl.ds(g * width, width)],
                dst_ref=buf.at[pl.ds(0, RIM), :],
                send_sem=rim_sem.at[index, g],
                recv_sem=recv_sem.at[4, index],
                device_id=(following, g),
                device_id_type=MESH,
            )
            for g in range(GROUPS)
        ]

    k_rims = rim_copies(0, k_in, kbuf, 256)
    v_rims = rim_copies(1, v_in, vbuf, 512)
    q_rims = rim_copies(2, q_in, qbuf, 256)

    def start_rims(rims):
        @pl.when(z == GROUPS - 1)
        def _():
            for rim in rims:
                rim.start()

    start_rims(k_rims)
    for copy in k_copies:
        copy.start()

    copies[0].wait()
    copies[1].wait()
    upto = jnp.where(rows <= cols, 1.0, 0.0)[:TOK, :TOK].astype(BF16)
    sums = dot(ld[...], upto)
    both = jnp.concatenate([ws[...].astype(F32), sums], axis=0)
    both = jnp.concatenate([both, both], axis=1)
    for g in range(GROUPS):
        gb_send[g] = jnp.concatenate(
            [both[HEADS * g : HEADS * g + HEADS], both[32 + HEADS * g : 32 + HEADS * g + HEADS]], axis=0
        )
    start_rims(v_rims)
    for copy in g_copies + v_copies:
        copy.start()
    gb_recv[z] = gb_send[z]

    copies[6].wait()
    gain = jnp.concatenate([gain_ref[...]] * HEADS, axis=1)

    def gate_body(g, carry):
        here = pl.ds(pl.multiple_of(g * 512, 512), 512)
        gating[:, here] = silu(gate[:, here].astype(F32)) * gain
        return carry

    lax.fori_loop(0, GROUPS, gate_body, 0)

    def arrived(own, others):
        own.wait()
        for copy in others:
            copy.wait_recv()

    def rim_arrived(rim, buf):
        rim.wait_recv()

        @pl.when(s == 0)
        def _():
            buf[pl.ds(0, RIM), :] = jnp.zeros((RIM, buf.shape[1]), BF16)

    def chunk_scales(c):
        first, second = gb_recv[2 * c], gb_recv[2 * c + 1]
        lane = lax.broadcasted_iota(jnp.int32, (8, C), 1)
        sub = lax.broadcasted_iota(jnp.int32, (8, C), 0)
        carry = jnp.where(sub >= HEADS, first[:, TOK - 1 : TOK], 0.0)
        across = jnp.where(lane < TOK, first, second + carry)
        return across, across.T

    copies[2].wait()
    for copy in g_copies:
        copy.wait_recv()
    arrived(copies[3], k_copies)
    taps_k = wbuf[:, pl.ds(pl.multiple_of(2048 + z * 256, 256), 256)].astype(F32)

    def key_body(i, carry):
        @pl.when(i == CHUNKS // PAIR - 1)
        def _():
            rim_arrived(k_rims[0], kbuf)

        units = []
        for n in range(PAIR):
            c = lax.rem(i * PAIR + PAIR + n, CHUNKS)
            start = pl.multiple_of(c * C, C)
            keys = conv(kbuf, start, taps_k)
            kc[pl.ds(start, C), :] = keys
            across, down = chunk_scales(c)
            for kh in range(2):
                key = keys[:, kh * D : (kh + 1) * D]
                kk = dot(key, key, NT)
                diagonal = jnp.where(eye, kk, 0.0)
                s_col = lax.rsqrt(jnp.sum(diagonal, axis=1, keepdims=True) + EPSILON)
                s_row = lax.rsqrt(jnp.sum(diagonal, axis=0, keepdims=True) + EPSILON)
                for j in range(2):
                    h = kh * 2 + j
                    b_col, c_col = down[:, h : h + 1], down[:, HEADS + h : HEADS + h + 1]
                    b_row, c_row = across[h : h + 1], across[HEADS + h : HEADS + h + 1]
                    end = c_row[:, C - 1 : C]
                    fade = jnp.where(tril, jnp.exp(jnp.where(tril, c_col - c_row, 0.0)), 0.0) * s_row
                    fs[h, pl.ds(start, C), :] = fade
                    lower = jnp.where(strict, kk * fade * (s_col * b_col), 0.0)
                    units.append((
                        h, c, pl.ds(start, C), key, lower, b_row, s_row * jnp.exp(c_row),
                        s_col * jnp.exp(end - c_col), jnp.exp(end),
                    ))
        ts = unit_inverses([unit[4] for unit in units], rows, cols)
        ts = [t * unit[5] for t, unit in zip(ts, units)]
        for t, unit in zip(ts, units):
            tinv[unit[0], unit[2], :] = t
        erases = [mm2l(t * unit[6], unit[3]) for t, unit in zip(ts, units)]
        for erase, unit in zip(erases, units):
            ew[unit[0], unit[2], pl.ds(0, D)] = erase
        takens = [mm2r(unit[3], erase * unit[7], TN) for erase, unit in zip(erases, units)]
        for taken, unit in zip(takens, units):
            mc[unit[0], unit[1]] = jnp.where(eye, unit[8], 0.0) - taken
        return carry

    lax.fori_loop(0, CHUNKS // PAIR, key_body, 0)

    identity = jnp.where(eye, 1.0, 0.0)
    left, right = pl.ds(0, D), pl.ds(D, D)
    for h in range(HEADS):
        pre[h, 0, :, left] = identity
        pre[h, 0, :, right] = jnp.zeros((D, D), F32)
    runnings = [mc[h, 0] for h in range(HEADS)]
    for c in range(1, CHUNKS):
        for h in range(HEADS):
            pre[h, c, :, left] = runnings[h]
        runnings = [mm3(mc[h, c], runnings[h]) for h in range(HEADS)]
    for h in range(HEADS):
        decay = gb_recv[0, HEADS + h : HEADS + h + 1, TOK - 1 : TOK]
        for g in range(1, GROUPS):
            decay = decay + gb_recv[g, HEADS + h : HEADS + h + 1, TOK - 1 : TOK]
        m_send[h] = pack_map(runnings[h], jnp.broadcast_to(jnp.exp(decay), (1, D)), eye)

    def unit_head(u):
        return u // 2

    def unit_half(u):
        return pl.ds(pl.multiple_of(lax.rem(u, 2) * 64, 64), 64)

    m_copies, a_copies, h_copies = [], [], []
    for d in [2, 6, 4, 3, 5, 1, 7]:
        u = at_line(d)
        target = y * LINE + u
        m_copies.append(to_seq(5, d, target, m_send.at[unit_head(u)], m_recv.at[l]))
        a_copies.append(to_seq(6, d, target, a_send.at[unit_head(u), unit_half(u), :], a_recv.at[l]))
        h_copies.append(to_seq(7, d, target, h_send.at[u], h_recv.at[l]))
    start_rims(q_rims)
    for copy in m_copies + q_copies:
        copy.start()
    m_recv[l] = m_send[unit_head(l)]

    arrived(copies[4], v_copies)
    taps_v = wbuf[:, pl.ds(pl.multiple_of(4096 + z * 512, 512), 512)].astype(F32)

    def value_body(i, carry):
        @pl.when(i == CHUNKS // PAIR - 1)
        def _():
            rim_arrived(v_rims[0], vbuf)

        for n in range(PAIR):
            c = lax.rem(i * PAIR + PAIR + n, CHUNKS)
            start = pl.multiple_of(c * C, C)
            block = pl.ds(start, C)
            values = conv(vbuf, start, taps_v)
            across, down = chunk_scales(c)
            for kh in range(2):
                key = kc[block, pl.ds(kh * D, D)]
                key32 = key.astype(F32)
                s_col = lax.rsqrt(jnp.sum(key32 * key32, axis=1, keepdims=True) + EPSILON)
                for j in range(2):
                    h = kh * 2 + j
                    c_col = down[:, HEADS + h : HEADS + h + 1]
                    end = across[HEADS + h : HEADS + h + 1, C - 1 : C]
                    write = mm2l(tinv[h, block, :], values[:, h * D : (h + 1) * D])
                    ew[h, block, pl.ds(D, D)] = write
                    ac[h, c] = mm2r(key, write * (s_col * jnp.exp(end - c_col)), TN)
        return carry

    lax.fori_loop(0, CHUNKS // PAIR, value_body, 0)
    runnings = [ac[h, 0] for h in range(HEADS)]
    for c in range(1, CHUNKS):
        for h in range(HEADS):
            pre[h, c, :, right] = runnings[h]
        runnings = [mm3(mc[h, c], runnings[h]) + ac[h, c] for h in range(HEADS)]
    for h in range(HEADS):
        a_send[h] = runnings[h].T.astype(BF16)
    for copy in a_copies:
        copy.start()
    a_recv[l] = a_send[unit_head(l), unit_half(l), :]

    for copy in m_copies:
        copy.wait_recv()
    m, f_total = [], None
    for i in range(LINE):
        unpacked, f_row = unpack_map(m_recv[i], eye)
        maps[i] = unpacked
        m.append(unpacked)
        f_total = f_row if f_total is None else f_total * f_row
    m01, m23, m45, m67 = mm3(m[1], m[0]), mm3(m[3], m[2]), mm3(m[5], m[4]), mm3(m[7], m[6])
    m03, m47 = mm3(m23, m01), mm3(m67, m45)
    m12, m46 = mm3(m23, m[1]), mm3(m[6], m45)
    ym_send[...] = pack_map(mm3(m47, m03), f_total, eye)
    mpre[1], mpre[2], mpre[3], mpre[4] = m[0], m01, mm3(m[2], m01), m03
    mpre[5], mpre[6], mpre[7] = mm3(m[4], m03), mm3(m45, m03), mm3(m46, m03)
    msuf[6], msuf[5], msuf[4], msuf[3] = m[7], m67, mm3(m67, m[5]), m47
    msuf[2], msuf[1], msuf[0] = mm3(m47, m[3]), mm3(m47, m23), mm3(m47, m12)
    mpair[0], mpair[1] = m23, m45
    ym_copies, ya_copies = [], []
    for d in range(1, LINES):
        target = lax.rem(y + d, LINES) * LINE + l
        ym_copies.append(to_seq(8, d, target, ym_send, ym_recv.at[d - 1]))
        ya_copies.append(to_seq(9, d, target, ya_send, ya_recv.at[d - 1]))

    def start_later(across):
        for d in range(1, LINES):

            @pl.when(y + d < LINES)
            def _(d=d):
                across[d - 1].start()

    def wait_earlier(across):
        for d in range(1, LINES):

            @pl.when(y >= d)
            def _(d=d):
                across[d - 1].wait_recv()

    start_later(ym_copies)
    for copy in a_copies:
        copy.wait_recv()
    adds = [a_recv[i] for i in range(LINE)]
    total = adds[LINE - 1].astype(F32)
    for i in range(LINE - 1):
        total = total + mm2r(adds[i], msuf[i], NT)
    ya_send[...] = total
    start_later(ya_copies)

    apre[1] = adds[0].astype(F32)
    apre[2] = mm2r(adds[0], maps[1], NT) + adds[1].astype(F32)
    apre[3] = mm3(apre[2], maps[2], NT) + adds[2].astype(F32)
    apre[4] = mm3(apre[2], mpair[0], NT) + (mm2r(adds[2], maps[3], NT) + adds[3].astype(F32))
    apre[5] = mm3(apre[4], maps[4], NT) + adds[4].astype(F32)
    apre[6] = mm3(apre[4], mpair[1], NT) + (mm2r(adds[4], maps[5], NT) + adds[5].astype(F32))
    apre[7] = mm3(apre[6], maps[6], NT) + adds[6].astype(F32)

    wait_earlier(ym_copies)
    line_one = jnp.where(y >= 1, unpack_map(ym_recv[0], eye)[0], 0.0)
    line_two = jnp.where(y >= 2, mm3(line_one, unpack_map(ym_recv[1], eye)[0]), 0.0)
    wait_earlier(ya_copies)
    entering = jnp.where(y >= 1, ya_recv[0], 0.0)
    entering = entering + jnp.where(y >= 2, mm3(ya_recv[1], line_one, NT), 0.0)
    entering = entering + jnp.where(y >= 3, mm3(ya_recv[2], line_two, NT), 0.0)
    h_send[0] = entering.astype(BF16)
    for i in range(1, LINE):
        h_send[i] = (mm3(entering, mpre[i], NT) + apre[i]).astype(BF16)
    for copy in h_copies:
        copy.start()
    h_recv[l] = h_send[l]

    arrived(copies[5], q_copies)
    taps_q = wbuf[:, pl.ds(pl.multiple_of(z * 256, 256), 256)].astype(F32)

    def query_body(i, carry):
        c = lax.rem(i + 1, CHUNKS)

        @pl.when(i == CHUNKS - 1)
        def _():
            rim_arrived(q_rims[0], qbuf)

        start = pl.multiple_of(c * C, C)
        block = pl.ds(start, C)
        queries = conv(qbuf, start, taps_q)
        across, down = chunk_scales(c)
        for kh in range(2):
            key = kc[block, pl.ds(kh * D, D)]
            query = queries[:, kh * D : (kh + 1) * D]
            query32 = query.astype(F32)
            s_col = lax.rsqrt(jnp.sum(query32 * query32, axis=1, keepdims=True) + EPSILON) * (D**-0.5)
            qk = dot(query, key, NT) * s_col
            for j in range(2):
                h = kh * 2 + j
                c_col = down[:, HEADS + h : HEADS + h + 1]
                inner = mm3(qk * fs[h, block, :], ew[h, block, :])
                reads = query32 * (s_col * jnp.exp(c_col)) - inner[:, :D]
                outer = mm3(reads, pre[h, c])
                pb[h, block, left] = outer[:, :D]
                pb[h, block, right] = outer[:, D:] + inner[:, D:]
        return carry

    lax.fori_loop(0, CHUNKS, query_body, 0)

    for copy in h_copies:
        copy.wait_recv()
    def far(i):
        half = i // 2
        return 4 + half - lax.rem(i, 2) * ((i + 1) // 2 + half)

    def out_copy(d):
        return to_head(10, d, o_send.at[at_head(d)], o_recv.at[z])

    def out_rows(t):
        block = pl.ds(pl.multiple_of(t * TOK, TOK), TOK)
        for h in range(HEADS):
            state = jnp.concatenate([h_recv[2 * h], h_recv[2 * h + 1]], axis=0)
            o = mm2l(pb[h, block, left], state, NT) + pb[h, block, right]
            o_send[t, :, pl.ds(h * D, D)] = o.astype(BF16)

    def out_body(i, carry):
        d = far(i)
        out_rows(at_head(d))

        @pl.when(i < GROUPS - 1)
        def _():
            out_copy(d).start()

        return carry

    lax.fori_loop(0, GROUPS, out_body, 0)
    o_recv[z] = o_send[z]

    def norm(g):
        for h in range(HEADS):
            a = o_recv[g, :, pl.ds(h * D, D)].astype(F32)
            a = a * lax.rsqrt(jnp.mean(a * a, axis=1, keepdims=True) + EPSILON)
            here = pl.ds(pl.multiple_of(g * 512 + h * D, D), D)
            out_ref[:, here] = (a * gating[:, here]).astype(BF16)

    def norm_body(i, carry):
        d = far(lax.rem(i + GROUPS - 1, GROUPS))

        @pl.when(i > 0)
        def _():
            out_copy(d).wait_recv()

        norm(lax.rem(z + GROUPS - d, GROUPS))
        return carry

    lax.fori_loop(0, GROUPS, norm_body, 0)

    def sent_body(i, carry):
        out_copy(far(i)).wait_send()
        return carry

    lax.fori_loop(0, GROUPS - 1, sent_body, 0)
    for copy in g_copies + k_copies + v_copies + q_copies + m_copies + a_copies + h_copies:
        copy.wait_send()

    @pl.when(z == GROUPS - 1)
    def _():
        for rim in k_rims + v_rims + q_rims:
            rim.wait_send()

    for d in range(1, LINES):

        @pl.when(y + d < LINES)
        def _(d=d):
            ym_copies[d - 1].wait_send()
            ya_copies[d - 1].wait_send()


def local(query_in, key_in, value_in, gate_in, write_strength, log_decay, conv_weight, norm_gain):
    anywhere = pl.BlockSpec(memory_space=pl.ANY)
    vmem = pl.BlockSpec(memory_space=pltpu.VMEM)
    return pl.pallas_call(
        kernel,
        out_shape=jax.ShapeDtypeStruct((TOK, 4096), BF16),
        in_specs=[anywhere] * 7 + [vmem],
        out_specs=vmem,
        scratch_shapes=[
            pltpu.VMEM((RIM + ROWS, 256), BF16),
            pltpu.VMEM((RIM + ROWS, 256), BF16),
            pltpu.VMEM((RIM + ROWS, 512), BF16),
            pltpu.VMEM((TOK, 4096), BF16),
            pltpu.VMEM((TOK, 4096), F32),
            pltpu.VMEM((32, TOK), BF16),
            pltpu.VMEM((32, TOK), BF16),
            pltpu.VMEM((4, 8192), BF16),
            pltpu.VMEM((GROUPS, 8, C), F32),
            pltpu.VMEM((GROUPS, 8, C), F32),
            pltpu.VMEM((ROWS, 256), BF16),
            pltpu.VMEM((HEADS, ROWS, C), F32),
            pltpu.VMEM((HEADS, ROWS, C), F32),
            pltpu.VMEM((HEADS, ROWS, 2 * D), F32),
            pltpu.VMEM((HEADS, CHUNKS, D, D), F32),
            pltpu.VMEM((HEADS, CHUNKS, D, D), F32),
            pltpu.VMEM((HEADS, CHUNKS, D, 2 * D), F32),
            pltpu.VMEM((HEADS, D + RIM, D), BF16),
            pltpu.VMEM((HEADS, D, D), BF16),
            pltpu.VMEM((LINE, D + RIM, D), BF16),
            pltpu.VMEM((LINE, D, D), F32),
            pltpu.VMEM((LINE, 64, D), BF16),
            pltpu.VMEM((LINE, D, D), F32),
            pltpu.VMEM((LINE, D, D), F32),
            pltpu.VMEM((2, D, D), F32),
            pltpu.VMEM((LINE, 64, D), F32),
            pltpu.VMEM((D + RIM, D), BF16),
            pltpu.VMEM((64, D), F32),
            pltpu.VMEM((LINES - 1, D + RIM, D), BF16),
            pltpu.VMEM((LINES - 1, 64, D), F32),
            pltpu.VMEM((LINE, 64, D), BF16),
            pltpu.VMEM((LINE, 64, D), BF16),
            pltpu.VMEM((HEADS, ROWS, 2 * D), F32),
            pltpu.VMEM((GROUPS, TOK, 512), BF16),
            pltpu.VMEM((GROUPS, TOK, 512), BF16),
            pltpu.SemaphoreType.DMA((7,)),
            pltpu.SemaphoreType.DMA((11, 8)),
            pltpu.SemaphoreType.DMA((11, 8)),
            pltpu.SemaphoreType.DMA((3, 8)),
        ],
        compiler_params=pltpu.CompilerParams(
            collective_id=0, has_side_effects=True, vmem_limit_bytes=60 * 1024 * 1024
        ),
    )(
        query_in, key_in, value_in, gate_in, write_strength.T, log_decay.T, conv_weight, norm_gain.reshape(1, D)
    )


def solution(mesh):
    rows = P(("seq", "head"), None)
    return jax.shard_map(
        local,
        mesh=mesh,
        in_specs=(rows, rows, rows, rows, rows, rows, P(), P()),
        out_specs=rows,
        check_vma=False,
    )
```

```python
import functools

import jax
import jax.numpy as jnp
from jax import lax
from jax.experimental import pallas as pl
from jax.experimental.pallas import tpu as pltpu
from jax.sharding import PartitionSpec as P

MESH = pl.DeviceIdType.MESH
F32 = jnp.float32
BF16 = jnp.bfloat16
EPSILON = 1e-06

GROUPS = 8
TOK = 64
LINE = 8
LINES = 4
SEQ = LINE * LINES
HEADS = 4
D = 128
C = 128
ROWS = TOK * GROUPS
CHUNKS = ROWS // C
RIM = 16
PAIR = 2

NN = (((1,), (0,)), ((), ()))
NT = (((1,), (1,)), ((), ()))
TN = (((0,), (0,)), ((), ()))


def dot(a, b, dims=NN):
    return lax.dot_general(a, b, dims, preferred_element_type=F32)


def split(x):
    high = x.astype(BF16)
    return high, (x - high.astype(F32)).astype(BF16)


def beside(b1, b2, dims):
    return jnp.concatenate([b1, b2], axis=0 if dims == NT else 1)


def mm2l(a, b, dims=NN):
    a1, a2 = split(a)
    axis = 1 if dims == NT else 0
    return dot(jnp.concatenate([a1, a2], axis=1), jnp.concatenate([b, b], axis=axis), dims)


def mm2r(a, b, dims=NN):
    b1, b2 = split(b)
    both = dot(a, beside(b1, b2, dims), dims)
    half = both.shape[1] // 2
    return both[:, :half] + both[:, half:]


def mm3(a, b, dims=NN):
    a1, a2 = split(a)
    b1, b2 = split(b)
    if b.shape[0 if dims == NT else 1] > D:
        axis = 1 if dims == NT else 0
        main = dot(jnp.concatenate([a1, a2], axis=1), jnp.concatenate([b1, b1], axis=axis), dims)
        return main + dot(a1, b2, dims)
    both = dot(a1, beside(b1, b2, dims), dims)
    half = both.shape[1] // 2
    return both[:, :half] + both[:, half:] + dot(a2, b1, dims)


def pack_map(m, f_row, eye):
    sub = lax.broadcasted_iota(jnp.int32, (RIM, D), 0)
    f1 = f_row.astype(BF16).astype(F32)
    f2 = (f_row - f1).astype(BF16).astype(F32)
    pieces = jnp.where(sub == 0, f1, jnp.where(sub == 1, f2, jnp.where(sub == 2, f_row - f1 - f2, 0.0)))
    return jnp.concatenate([m - jnp.where(eye, f_row, 0.0), pieces], axis=0).astype(BF16)


def unpack_map(packed, eye):
    f_row = jnp.sum(packed[D:].astype(F32), axis=0, keepdims=True)
    return packed[:D].astype(F32) + jnp.where(eye, f_row, 0.0), f_row


def silu(x):
    return x / (1.0 + jnp.exp(-x))


def conv(buf, start, taps):
    x = buf[pl.ds(start, C + RIM), :].astype(F32)
    total = x[RIM - 3 : RIM - 3 + C] * taps[0:1]
    for j in range(1, 4):
        total = total + x[RIM - 3 + j : RIM - 3 + j + C] * taps[j : j + 1]
    return silu(total).astype(BF16)


def odd_blocks(x, size):
    return jnp.concatenate([x[i : i + size] for i in range(size, C, 2 * size)], axis=0)


def to_odd_blocks(x, size):
    zero = jnp.zeros((size, x.shape[1]), x.dtype)
    parts = []
    for i in range(0, C // 2, size):
        parts += [zero, x[i : i + size]]
    return jnp.concatenate(parts, axis=0)


def unit_inverses(lowers, rows, cols):
    identity = jnp.where(rows == cols, 1.0, 0.0)
    base = (rows // 8) * 8
    ts = [identity.reshape(C // 8, 8, C)] * len(lowers)
    for j in range(7):
        picked = cols == base + j
        for n, lower in enumerate(lowers):
            factor = jnp.sum(jnp.where(picked, lower, 0.0), axis=1, keepdims=True).reshape(C // 8, 8, 1)
            ts[n] = ts[n] - factor * ts[n][:, j : j + 1, :]
    ts = [t.reshape(C, C) for t in ts]
    size = 8
    while size < C:
        below = odd_blocks(cols // size, size) == odd_blocks(rows // size, size) - 1
        parts = [jnp.where(below, odd_blocks(lower, size), 0.0).astype(BF16) for lower in lowers]
        firsts = [dot(part, t.astype(BF16)) for part, t in zip(parts, ts)]
        seconds = [
            dot(odd_blocks(t, size).astype(BF16), to_odd_blocks(first, size).astype(BF16))
            for t, first in zip(ts, firsts)
        ]
        ts = [t - to_odd_blocks(second, size) for t, second in zip(ts, seconds)]
        size *= 2
    rounded = [t.astype(BF16) for t in ts]
    misses = [identity - t.astype(F32) - mm2l(lower, t) for lower, t in zip(lowers, rounded)]
    return [t.astype(F32) + dot(t, miss.astype(BF16)) for t, miss in zip(rounded, misses)]


def kernel(
    q_in, k_in, v_in, gate_in, ws_in, ld_in, w_in, gain_ref, out_ref,
    qbuf, kbuf, vbuf, gate, gating, ws, ld, wbuf, gb_send, gb_recv,
    kc, fs, tinv, ew, mc, ac, pre, m_send, a_send, m_recv, maps, a_recv,
    mpre, msuf, mpair, apre, ym_send, ya_send, ym_recv, ya_recv, h_send, h_recv, pb, o_send, o_recv,
    local_sem, send_sem, recv_sem, rim_sem,
):
    s = lax.axis_index("seq")
    z = lax.axis_index("head")
    y = s // LINE
    l = lax.rem(s, LINE)

    def at_head(d):
        return lax.rem(z + d, GROUPS)

    def at_line(d):
        return lax.rem(l + d, LINE)

    barrier = pltpu.get_barrier_semaphore()
    for d in range(1, GROUPS):
        pl.semaphore_signal(barrier, inc=1, device_id=(s, at_head(d)), device_id_type=MESH)
    for d in range(1, LINE):
        pl.semaphore_signal(barrier, inc=1, device_id=(y * LINE + at_line(d), z), device_id_type=MESH)
    for d in range(1, LINES):
        pl.semaphore_signal(
            barrier, inc=1, device_id=(lax.rem(y + d, LINES) * LINE + l, z), device_id_type=MESH
        )
    pl.semaphore_signal(
        barrier, inc=1, device_id=(lax.rem(s + SEQ - 1, SEQ), GROUPS - 1), device_id_type=MESH
    )

    mine = pl.ds(pl.multiple_of(RIM + z * TOK, RIM), TOK)

    def own_columns(width):
        return pl.ds(pl.multiple_of(z * width, width), width)

    copies = [
        pltpu.make_async_copy(ws_in, ws, local_sem.at[0]),
        pltpu.make_async_copy(ld_in, ld, local_sem.at[1]),
        pltpu.make_async_copy(w_in, wbuf, local_sem.at[2]),
        pltpu.make_async_copy(k_in.at[:, own_columns(256)], kbuf.at[mine, :], local_sem.at[3]),
        pltpu.make_async_copy(v_in.at[:, own_columns(512)], vbuf.at[mine, :], local_sem.at[4]),
        pltpu.make_async_copy(q_in.at[:, own_columns(256)], qbuf.at[mine, :], local_sem.at[5]),
        pltpu.make_async_copy(gate_in, gate, local_sem.at[6]),
    ]
    for copy in copies[:4]:
        copy.start()

    rows = lax.broadcasted_iota(jnp.int32, (C, C), 0)
    cols = lax.broadcasted_iota(jnp.int32, (C, C), 1)
    eye = rows == cols
    tril = rows >= cols
    strict = rows > cols

    partners = GROUPS - 1 + LINE - 1 + LINES - 1

    @pl.when(z < GROUPS - 1)
    def _():
        pl.semaphore_wait(barrier, partners)

    @pl.when(z == GROUPS - 1)
    def _():
        pl.semaphore_wait(barrier, partners + GROUPS)

    def to_head(kind, d, src, dst):
        return pltpu.make_async_remote_copy(
            src_ref=src,
            dst_ref=dst,
            send_sem=send_sem.at[kind, d],
            recv_sem=recv_sem.at[kind, d],
            device_id=(s, at_head(d)),
            device_id_type=MESH,
        )

    def to_seq(kind, d, target, src, dst):
        return pltpu.make_async_remote_copy(
            src_ref=src,
            dst_ref=dst,
            send_sem=send_sem.at[kind, d],
            recv_sem=recv_sem.at[kind, d],
            device_id=(target, z),
            device_id_type=MESH,
        )

    def columns_to(d, width):
        return pl.ds(pl.multiple_of(at_head(d) * width, width), width)

    near = [1, 7, 2, 6, 3, 5, 4]
    k_copies = [to_head(1, d, k_in.at[:, columns_to(d, 256)], kbuf.at[mine, :]) for d in near]
    v_copies = [to_head(2, d, v_in.at[:, columns_to(d, 512)], vbuf.at[mine, :]) for d in near]
    q_copies = [to_head(3, d, q_in.at[:, columns_to(d, 256)], qbuf.at[mine, :]) for d in near]
    g_copies = [to_head(0, d, gb_send.at[at_head(d)], gb_recv.at[z]) for d in near]
    following = lax.rem(s + 1, SEQ)

    def rim_copies(index, source, buf, width):
        return [
            pltpu.make_async_remote_copy(
                src_ref=source.at[pl.ds(TOK - RIM, RIM), pl.ds(g * width, width)],
                dst_ref=buf.at[pl.ds(0, RIM), :],
                send_sem=rim_sem.at[index, g],
                recv_sem=recv_sem.at[4, index],
                device_id=(following, g),
                device_id_type=MESH,
            )
            for g in range(GROUPS)
        ]

    k_rims = rim_copies(0, k_in, kbuf, 256)
    v_rims = rim_copies(1, v_in, vbuf, 512)
    q_rims = rim_copies(2, q_in, qbuf, 256)

    def start_rims(rims):
        @pl.when(z == GROUPS - 1)
        def _():
            for rim in rims:
                rim.start()

    start_rims(k_rims)
    for copy in k_copies:
        copy.start()
    for copy in copies[4:]:
        copy.start()

    copies[0].wait()
    copies[1].wait()
    upto = jnp.where(rows <= cols, 1.0, 0.0)[:TOK, :TOK].astype(BF16)
    sums = dot(ld[...], upto)
    both = jnp.concatenate([ws[...].astype(F32), sums], axis=0)
    both = jnp.concatenate([both, both], axis=1)
    for g in range(GROUPS):
        gb_send[g] = jnp.concatenate(
            [both[HEADS * g : HEADS * g + HEADS], both[32 + HEADS * g : 32 + HEADS * g + HEADS]], axis=0
        )
    start_rims(v_rims)
    for copy in g_copies + v_copies:
        copy.start()
    gb_recv[z] = gb_send[z]

    copies[6].wait()
    gain = jnp.concatenate([gain_ref[...]] * HEADS, axis=1)

    def gate_body(g, carry):
        here = pl.ds(pl.multiple_of(g * 512, 512), 512)
        gating[:, here] = silu(gate[:, here].astype(F32)) * gain
        return carry

    lax.fori_loop(0, GROUPS, gate_body, 0)

    def arrived(own, others):
        own.wait()
        for copy in others:
            copy.wait_recv()

    def rim_arrived(rim, buf):
        rim.wait_recv()

        @pl.when(s == 0)
        def _():
            buf[pl.ds(0, RIM), :] = jnp.zeros((RIM, buf.shape[1]), BF16)

    def chunk_scales(c):
        first, second = gb_recv[2 * c], gb_recv[2 * c + 1]
        lane = lax.broadcasted_iota(jnp.int32, (8, C), 1)
        sub = lax.broadcasted_iota(jnp.int32, (8, C), 0)
        carry = jnp.where(sub >= HEADS, first[:, TOK - 1 : TOK], 0.0)
        across = jnp.where(lane < TOK, first, second + carry)
        return across, across.T

    copies[2].wait()
    for copy in g_copies:
        copy.wait_recv()
    arrived(copies[3], k_copies)
    taps_k = wbuf[:, pl.ds(pl.multiple_of(2048 + z * 256, 256), 256)].astype(F32)

    def key_body(i, carry):
        @pl.when(i == CHUNKS // PAIR - 1)
        def _():
            rim_arrived(k_rims[0], kbuf)

        units = []
        for n in range(PAIR):
            c = lax.rem(i * PAIR + PAIR + n, CHUNKS)
            start = pl.multiple_of(c * C, C)
            keys = conv(kbuf, start, taps_k)
            kc[pl.ds(start, C), :] = keys
            across, down = chunk_scales(c)
            for kh in range(2):
                key = keys[:, kh * D : (kh + 1) * D]
                kk = dot(key, key, NT)
                diagonal = jnp.where(eye, kk, 0.0)
                s_col = lax.rsqrt(jnp.sum(diagonal, axis=1, keepdims=True) + EPSILON)
                s_row = lax.rsqrt(jnp.sum(diagonal, axis=0, keepdims=True) + EPSILON)
                for j in range(2):
                    h = kh * 2 + j
                    b_col, c_col = down[:, h : h + 1], down[:, HEADS + h : HEADS + h + 1]
                    b_row, c_row = across[h : h + 1], across[HEADS + h : HEADS + h + 1]
                    end = c_row[:, C - 1 : C]
                    fade = jnp.where(tril, jnp.exp(jnp.where(tril, c_col - c_row, 0.0)), 0.0) * s_row
                    fs[h, pl.ds(start, C), :] = fade
                    lower = jnp.where(strict, kk * fade * (s_col * b_col), 0.0)
                    units.append((
                        h, c, pl.ds(start, C), key, lower, b_row, s_row * jnp.exp(c_row),
                        s_col * jnp.exp(end - c_col), jnp.exp(end),
                    ))
        ts = unit_inverses([unit[4] for unit in units], rows, cols)
        ts = [t * unit[5] for t, unit in zip(ts, units)]
        for t, unit in zip(ts, units):
            tinv[unit[0], unit[2], :] = t
        erases = [mm2l(t * unit[6], unit[3]) for t, unit in zip(ts, units)]
        for erase, unit in zip(erases, units):
            ew[unit[0], unit[2], pl.ds(0, D)] = erase
        takens = [mm2r(unit[3], erase * unit[7], TN) for erase, unit in zip(erases, units)]
        for taken, unit in zip(takens, units):
            mc[unit[0], unit[1]] = jnp.where(eye, unit[8], 0.0) - taken
        return carry

    lax.fori_loop(0, CHUNKS // PAIR, key_body, 0)

    identity = jnp.where(eye, 1.0, 0.0)
    left, right = pl.ds(0, D), pl.ds(D, D)
    for h in range(HEADS):
        pre[h, 0, :, left] = identity
        pre[h, 0, :, right] = jnp.zeros((D, D), F32)
    runnings = [mc[h, 0] for h in range(HEADS)]
    for c in range(1, CHUNKS):
        for h in range(HEADS):
            pre[h, c, :, left] = runnings[h]
        runnings = [mm3(mc[h, c], runnings[h]) for h in range(HEADS)]
    for h in range(HEADS):
        decay = gb_recv[0, HEADS + h : HEADS + h + 1, TOK - 1 : TOK]
        for g in range(1, GROUPS):
            decay = decay + gb_recv[g, HEADS + h : HEADS + h + 1, TOK - 1 : TOK]
        m_send[h] = pack_map(runnings[h], jnp.broadcast_to(jnp.exp(decay), (1, D)), eye)

    def unit_head(u):
        return u // 2

    def unit_half(u):
        return pl.ds(pl.multiple_of(lax.rem(u, 2) * 64, 64), 64)

    m_copies, a_copies, h_copies = [], [], []
    for d in [2, 6, 4, 3, 5, 1, 7]:
        u = at_line(d)
        target = y * LINE + u
        m_copies.append(to_seq(5, d, target, m_send.at[unit_head(u)], m_recv.at[l]))
        a_copies.append(to_seq(6, d, target, a_send.at[unit_head(u), unit_half(u), :], a_recv.at[l]))
        h_copies.append(to_seq(7, d, target, h_send.at[u], h_recv.at[l]))
    start_rims(q_rims)
    for copy in m_copies + q_copies:
        copy.start()
    m_recv[l] = m_send[unit_head(l)]

    arrived(copies[4], v_copies)
    taps_v = wbuf[:, pl.ds(pl.multiple_of(4096 + z * 512, 512), 512)].astype(F32)

    def value_body(i, carry):
        @pl.when(i == CHUNKS // PAIR - 1)
        def _():
            rim_arrived(v_rims[0], vbuf)

        for n in range(PAIR):
            c = lax.rem(i * PAIR + PAIR + n, CHUNKS)
            start = pl.multiple_of(c * C, C)
            block = pl.ds(start, C)
            values = conv(vbuf, start, taps_v)
            across, down = chunk_scales(c)
            for kh in range(2):
                key = kc[block, pl.ds(kh * D, D)]
                key32 = key.astype(F32)
                s_col = lax.rsqrt(jnp.sum(key32 * key32, axis=1, keepdims=True) + EPSILON)
                for j in range(2):
                    h = kh * 2 + j
                    c_col = down[:, HEADS + h : HEADS + h + 1]
                    end = across[HEADS + h : HEADS + h + 1, C - 1 : C]
                    write = mm2l(tinv[h, block, :], values[:, h * D : (h + 1) * D])
                    ew[h, block, pl.ds(D, D)] = write
                    ac[h, c] = mm2r(key, write * (s_col * jnp.exp(end - c_col)), TN)
        return carry

    lax.fori_loop(0, CHUNKS // PAIR, value_body, 0)
    runnings = [ac[h, 0] for h in range(HEADS)]
    for c in range(1, CHUNKS):
        for h in range(HEADS):
            pre[h, c, :, right] = runnings[h]
        runnings = [mm3(mc[h, c], runnings[h]) + ac[h, c] for h in range(HEADS)]
    for h in range(HEADS):
        a_send[h] = runnings[h].T.astype(BF16)
    for copy in a_copies:
        copy.start()
    a_recv[l] = a_send[unit_head(l), unit_half(l), :]

    for copy in m_copies:
        copy.wait_recv()
    m, f_total = [], None
    for i in range(LINE):
        unpacked, f_row = unpack_map(m_recv[i], eye)
        maps[i] = unpacked
        m.append(unpacked)
        f_total = f_row if f_total is None else f_total * f_row
    m01, m23, m45, m67 = mm3(m[1], m[0]), mm3(m[3], m[2]), mm3(m[5], m[4]), mm3(m[7], m[6])
    m03, m47 = mm3(m23, m01), mm3(m67, m45)
    m12, m46 = mm3(m23, m[1]), mm3(m[6], m45)
    ym_send[...] = pack_map(mm3(m47, m03), f_total, eye)
    mpre[1], mpre[2], mpre[3], mpre[4] = m[0], m01, mm3(m[2], m01), m03
    mpre[5], mpre[6], mpre[7] = mm3(m[4], m03), mm3(m45, m03), mm3(m46, m03)
    msuf[6], msuf[5], msuf[4], msuf[3] = m[7], m67, mm3(m67, m[5]), m47
    msuf[2], msuf[1], msuf[0] = mm3(m47, m[3]), mm3(m47, m23), mm3(m47, m12)
    mpair[0], mpair[1] = m23, m45
    ym_copies, ya_copies = [], []
    for d in range(1, LINES):
        target = lax.rem(y + d, LINES) * LINE + l
        ym_copies.append(to_seq(8, d, target, ym_send, ym_recv.at[d - 1]))
        ya_copies.append(to_seq(9, d, target, ya_send, ya_recv.at[d - 1]))

    def start_later(across):
        for d in range(1, LINES):

            @pl.when(y + d < LINES)
            def _(d=d):
                across[d - 1].start()

    def wait_earlier(across):
        for d in range(1, LINES):

            @pl.when(y >= d)
            def _(d=d):
                across[d - 1].wait_recv()

    start_later(ym_copies)
    for copy in a_copies:
        copy.wait_recv()
    adds = [a_recv[i] for i in range(LINE)]
    total = adds[LINE - 1].astype(F32)
    for i in range(LINE - 1):
        total = total + mm2r(adds[i], msuf[i], NT)
    ya_send[...] = total
    start_later(ya_copies)

    apre[1] = adds[0].astype(F32)
    apre[2] = mm2r(adds[0], maps[1], NT) + adds[1].astype(F32)
    apre[3] = mm3(apre[2], maps[2], NT) + adds[2].astype(F32)
    apre[4] = mm3(apre[2], mpair[0], NT) + (mm2r(adds[2], maps[3], NT) + adds[3].astype(F32))
    apre[5] = mm3(apre[4], maps[4], NT) + adds[4].astype(F32)
    apre[6] = mm3(apre[4], mpair[1], NT) + (mm2r(adds[4], maps[5], NT) + adds[5].astype(F32))
    apre[7] = mm3(apre[6], maps[6], NT) + adds[6].astype(F32)

    wait_earlier(ym_copies)
    line_one = jnp.where(y >= 1, unpack_map(ym_recv[0], eye)[0], 0.0)
    line_two = jnp.where(y >= 2, mm3(line_one, unpack_map(ym_recv[1], eye)[0]), 0.0)
    wait_earlier(ya_copies)
    entering = jnp.where(y >= 1, ya_recv[0], 0.0)
    entering = entering + jnp.where(y >= 2, mm3(ya_recv[1], line_one, NT), 0.0)
    entering = entering + jnp.where(y >= 3, mm3(ya_recv[2], line_two, NT), 0.0)
    h_send[0] = entering.astype(BF16)
    for i in range(1, LINE):
        h_send[i] = (mm3(entering, mpre[i], NT) + apre[i]).astype(BF16)
    for copy in h_copies:
        copy.start()
    h_recv[l] = h_send[l]

    arrived(copies[5], q_copies)
    taps_q = wbuf[:, pl.ds(pl.multiple_of(z * 256, 256), 256)].astype(F32)

    def query_body(i, carry):
        c = lax.rem(i + 1, CHUNKS)

        @pl.when(i == CHUNKS - 1)
        def _():
            rim_arrived(q_rims[0], qbuf)

        start = pl.multiple_of(c * C, C)
        block = pl.ds(start, C)
        queries = conv(qbuf, start, taps_q)
        across, down = chunk_scales(c)
        for kh in range(2):
            key = kc[block, pl.ds(kh * D, D)]
            query = queries[:, kh * D : (kh + 1) * D]
            query32 = query.astype(F32)
            s_col = lax.rsqrt(jnp.sum(query32 * query32, axis=1, keepdims=True) + EPSILON) * (D**-0.5)
            qk = dot(query, key, NT) * s_col
            for j in range(2):
                h = kh * 2 + j
                c_col = down[:, HEADS + h : HEADS + h + 1]
                inner = mm3(qk * fs[h, block, :], ew[h, block, :])
                reads = query32 * (s_col * jnp.exp(c_col)) - inner[:, :D]
                outer = mm3(reads, pre[h, c])
                pb[h, block, left] = outer[:, :D]
                pb[h, block, right] = outer[:, D:] + inner[:, D:]
        return carry

    lax.fori_loop(0, CHUNKS, query_body, 0)

    for copy in h_copies:
        copy.wait_recv()
    def far(i):
        half = i // 2
        return 4 + half - lax.rem(i, 2) * ((i + 1) // 2 + half)

    def out_copy(d):
        return to_head(10, d, o_send.at[at_head(d)], o_recv.at[z])

    def out_rows(t):
        block = pl.ds(pl.multiple_of(t * TOK, TOK), TOK)
        for h in range(HEADS):
            state = jnp.concatenate([h_recv[2 * h], h_recv[2 * h + 1]], axis=0)
            o = mm2l(pb[h, block, left], state, NT) + pb[h, block, right]
            o_send[t, :, pl.ds(h * D, D)] = o.astype(BF16)

    def out_body(i, carry):
        d = far(i)
        out_rows(at_head(d))

        @pl.when(i < GROUPS - 1)
        def _():
            out_copy(d).start()

        return carry

    lax.fori_loop(0, GROUPS, out_body, 0)
    o_recv[z] = o_send[z]

    def norm(g):
        for h in range(HEADS):
            a = o_recv[g, :, pl.ds(h * D, D)].astype(F32)
            a = a * lax.rsqrt(jnp.mean(a * a, axis=1, keepdims=True) + EPSILON)
            here = pl.ds(pl.multiple_of(g * 512 + h * D, D), D)
            out_ref[:, here] = (a * gating[:, here]).astype(BF16)

    def norm_body(i, carry):
        d = far(lax.rem(i + GROUPS - 1, GROUPS))

        @pl.when(i > 0)
        def _():
            out_copy(d).wait_recv()

        norm(lax.rem(z + GROUPS - d, GROUPS))
        return carry

    lax.fori_loop(0, GROUPS, norm_body, 0)

    def sent_body(i, carry):
        out_copy(far(i)).wait_send()
        return carry

    lax.fori_loop(0, GROUPS - 1, sent_body, 0)
    for copy in g_copies + k_copies + v_copies + q_copies + m_copies + a_copies + h_copies:
        copy.wait_send()

    @pl.when(z == GROUPS - 1)
    def _():
        for rim in k_rims + v_rims + q_rims:
            rim.wait_send()

    for d in range(1, LINES):

        @pl.when(y + d < LINES)
        def _(d=d):
            ym_copies[d - 1].wait_send()
            ya_copies[d - 1].wait_send()


def local(query_in, key_in, value_in, gate_in, write_strength, log_decay, conv_weight, norm_gain):
    anywhere = pl.BlockSpec(memory_space=pl.ANY)
    vmem = pl.BlockSpec(memory_space=pltpu.VMEM)
    return pl.pallas_call(
        kernel,
        out_shape=jax.ShapeDtypeStruct((TOK, 4096), BF16),
        in_specs=[anywhere] * 7 + [vmem],
        out_specs=vmem,
        scratch_shapes=[
            pltpu.VMEM((RIM + ROWS, 256), BF16),
            pltpu.VMEM((RIM + ROWS, 256), BF16),
            pltpu.VMEM((RIM + ROWS, 512), BF16),
            pltpu.VMEM((TOK, 4096), BF16),
            pltpu.VMEM((TOK, 4096), F32),
            pltpu.VMEM((32, TOK), BF16),
            pltpu.VMEM((32, TOK), BF16),
            pltpu.VMEM((4, 8192), BF16),
            pltpu.VMEM((GROUPS, 8, C), F32),
            pltpu.VMEM((GROUPS, 8, C), F32),
            pltpu.VMEM((ROWS, 256), BF16),
            pltpu.VMEM((HEADS, ROWS, C), F32),
            pltpu.VMEM((HEADS, ROWS, C), F32),
            pltpu.VMEM((HEADS, ROWS, 2 * D), F32),
            pltpu.VMEM((HEADS, CHUNKS, D, D), F32),
            pltpu.VMEM((HEADS, CHUNKS, D, D), F32),
            pltpu.VMEM((HEADS, CHUNKS, D, 2 * D), F32),
            pltpu.VMEM((HEADS, D + RIM, D), BF16),
            pltpu.VMEM((HEADS, D, D), BF16),
            pltpu.VMEM((LINE, D + RIM, D), BF16),
            pltpu.VMEM((LINE, D, D), F32),
            pltpu.VMEM((LINE, 64, D), BF16),
            pltpu.VMEM((LINE, D, D), F32),
            pltpu.VMEM((LINE, D, D), F32),
            pltpu.VMEM((2, D, D), F32),
            pltpu.VMEM((LINE, 64, D), F32),
            pltpu.VMEM((D + RIM, D), BF16),
            pltpu.VMEM((64, D), F32),
            pltpu.VMEM((LINES - 1, D + RIM, D), BF16),
            pltpu.VMEM((LINES - 1, 64, D), F32),
            pltpu.VMEM((LINE, 64, D), BF16),
            pltpu.VMEM((LINE, 64, D), BF16),
            pltpu.VMEM((HEADS, ROWS, 2 * D), F32),
            pltpu.VMEM((GROUPS, TOK, 512), BF16),
            pltpu.VMEM((GROUPS, TOK, 512), BF16),
            pltpu.SemaphoreType.DMA((7,)),
            pltpu.SemaphoreType.DMA((11, 8)),
            pltpu.SemaphoreType.DMA((11, 8)),
            pltpu.SemaphoreType.DMA((3, 8)),
        ],
        compiler_params=pltpu.CompilerParams(
            collective_id=0, has_side_effects=True, vmem_limit_bytes=60 * 1024 * 1024
        ),
    )(
        query_in, key_in, value_in, gate_in, write_strength.T, log_decay.T, conv_weight, norm_gain.reshape(1, D)
    )


def solution(mesh):
    rows = P(("seq", "head"), None)
    return jax.shard_map(
        local,
        mesh=mesh,
        in_specs=(rows, rows, rows, rows, rows, rows, P(), P()),
        out_specs=rows,
        check_vma=False,
    )
```
